32 devices in a mesh: row: 4 (over z), chan: 8 (over y, x, core).
Axes of the slice: x: 2, y: 2, z: 4, core: 2. Of those that a mesh axis runs over, the one named last changes fastest.
Arguments:
- pair: bfloat16 [256, 256, 128], P('row', 'chan'), may hold values from -6 to 6
- tile_mask: int32 [64, 64], replicated, may hold values from 0 to 1, as said below
- in_gain: float32 [128], replicated, may hold values from 0.5 to 1.5
- in_shift: float32 [128], replicated, may hold values from -3 to 3
- left_gate: bfloat16 [128, 128], replicated, may hold values from -0.5 to 0.5
- left_proj: bfloat16 [128, 128], replicated, may hold values from -0.5 to 0.5
- right_gate: bfloat16 [128, 128], replicated, may hold values from -0.5 to 0.5
- right_proj: bfloat16 [128, 128], replicated, may hold values from -0.5 to 0.5
- out_gain: float32 [128], replicated, may hold values from 0.5 to 1.5
- out_shift: float32 [128], replicated, may hold values from -3 to 3
- out_gate: bfloat16 [128, 128], replicated, may hold values from -0.5 to 0.5
- out_proj: bfloat16 [128, 128], replicated, may hold values from -0.5 to 0.5
Outputs:
- updated: bfloat16 [256, 256, 128], P('row', 'chan')
The draws below stay inside these ranges and needn't reach their ends.
Inputs may be any that keep to these rules, and one draw needn't show every extreme that they name: tile_mask[p, q] = valid[p] * valid[q] for a 0/1 vector valid over the 64 tiles that is 1 on the first 32 tiles and, in the second half, 1 on a leading run of 16 to 32 tiles and 0 after it.
All inputs are finite; a program needn't handle non-finite values.
Results may differ from the reference program's by a relative error of at most 0.012.
Values may be sent and summed in bfloat16 or wider, within the bound.
A program may use at most 64 MiB of HBM per device.

```python
import jax
import jax.numpy as jnp
from jax import lax

C = 128
H = 128
TILES = 64
N = 256
TILE = 4


def draw_tile_mask(key, part):
    half_tiles = TILES // 2
    run_length = jax.random.randint(key, (), TILES // 4, half_tiles + 1)
    indices = jnp.arange(TILES, dtype=jnp.int32)
    valid = jnp.where(indices < half_tiles, 1, jnp.where(indices - half_tiles < run_length, 1, 0)).astype(jnp.int32)
    return valid[:, None] * valid[None, :]


def shard_levels(key, shape, split, smallest, top_value):
    def one(axis_at, parts):
        steps = jax.random.uniform(jax.random.fold_in(jax.random.fold_in(key, 6), axis_at), (parts,), jnp.float32, smallest / len(split), top_value / len(split))
        return jnp.repeat(jnp.exp(steps), shape[axis_at] // parts).reshape((-1,) + (1,) * (len(shape) - axis_at - 1))

    factor_of = one(*split[0])
    for cut in split[1:]:
        factor_of = factor_of * one(*cut)
    return factor_of


def gaussian(rng, dims, deviation, bound, cuts=(), kind=jnp.bfloat16):
    drawn = jax.random.normal(rng, dims, jnp.float32) * deviation
    if len(cuts) > 0:
        drawn = shard_levels(rng, dims, cuts, -0.22, 0.18) * drawn
    return jnp.clip(drawn, min=-bound, max=bound).astype(kind)


def setup_inputs(seed: int = 0) -> dict:
    keys = jax.random.split(jax.random.key(seed), 13)
    return {
        "pair": gaussian(keys[0], (N, N, C), 1.0, 6.0, ((0, 4), (1, 8))),
        "tile_mask": draw_tile_mask(jax.random.fold_in(keys[12], 71), 0),
        "in_gain": jnp.clip(1.0 + 0.1 * jax.random.normal(keys[2], (C,), jnp.float32), 0.5, 1.5),
        "in_shift": gaussian(keys[3], (C,), 0.5, 3.0, (), jnp.float32),
        "left_gate": gaussian(keys[4], (C, H), C ** -0.5, 0.5),
        "left_proj": gaussian(keys[5], (C, H), C ** -0.5, 0.5),
        "right_gate": gaussian(keys[6], (C, H), C ** -0.5, 0.5),
        "right_proj": gaussian(keys[7], (C, H), C ** -0.5, 0.5),
        "out_gain": jnp.clip(1.0 + 0.1 * jax.random.normal(keys[8], (H,), jnp.float32), 0.5, 1.5),
        "out_shift": gaussian(keys[9], (H,), 0.5, 3.0, (), jnp.float32),
        "out_gate": gaussian(keys[10], (C, C), C ** -0.5, 0.5),
        "out_proj": gaussian(keys[11], (H, C), H ** -0.5, 0.5),
    }


def layer_norm(values, gain, shift):
    average = lax.optimization_barrier(jnp.mean(values, axis=-1, keepdims=True))
    squares = lax.optimization_barrier(jnp.mean(values * values, axis=-1, keepdims=True))
    return (values - average) * lax.rsqrt(squares - average * average + 1e-05) * gain + shift

def reference(pair, tile_mask, in_gain, in_shift, left_gate, left_proj, right_gate, right_proj, out_gain, out_shift, out_gate, out_proj):
    normed = layer_norm(pair.astype(jnp.float32), in_gain, in_shift).astype(jnp.bfloat16)
    normed_f = normed.astype(jnp.float32)
    tile_ids = jnp.arange(N, dtype=jnp.int32) // TILE
    one_hot = (tile_ids[:, None] == jnp.arange(TILES, dtype=jnp.int32)[None, :]).astype(jnp.float32)
    pair_mask = jnp.dot(jnp.dot(one_hot, tile_mask.astype(jnp.float32), preferred_element_type=jnp.float32), one_hot.T, preferred_element_type=jnp.float32)

    def edges(gate_w, proj_w):
        gate_pre = jnp.einsum('ijc,ch->ijh', normed_f, gate_w.astype(jnp.float32))
        proj_pre = jnp.einsum('ijc,ch->ijh', normed_f, proj_w.astype(jnp.float32))
        return (pair_mask[:, :, None] * jax.nn.sigmoid(gate_pre) * proj_pre).astype(jnp.bfloat16)
    left = edges(left_gate, left_proj)
    right = edges(right_gate, right_proj)
    crossed = jnp.einsum('ikh,jkh->ijh', left.astype(jnp.float32), right.astype(jnp.float32)).astype(jnp.bfloat16)
    normed_x = layer_norm(crossed.astype(jnp.float32), out_gain, out_shift).astype(jnp.bfloat16)
    gating = jax.nn.sigmoid(jnp.einsum('ijc,cd->ijd', normed_f, out_gate.astype(jnp.float32)))
    projected = jnp.einsum('ijh,hd->ijd', normed_x.astype(jnp.float32), out_proj.astype(jnp.float32))
    return (gating * projected).astype(jnp.bfloat16)
```

```python
import functools
import math

import jax
import jax.numpy as jnp
from jax import lax
from jax.experimental import pallas as pl
from jax.experimental.pallas import tpu as pltpu
from jax.sharding import PartitionSpec as P

MESH = pl.DeviceIdType.MESH
F32 = jnp.float32
BF16 = jnp.bfloat16
epsilon = 1e-05


def contract(a, b, da, db):
    return lax.dot_general(a, b, (((da,), (db,)), ((), ())), preferred_element_type=F32)


def column(row_ref):
    width = row_ref.shape[1]
    return jnp.transpose(jnp.broadcast_to(row_ref[...], (width, width)))


def kernel(
    nr, nc, parts,
    pair, tile_mask, in_gain, in_shift, left_gate, left_proj, right_gate, right_proj,
    out_gain, out_shift, out_gate, out_proj,
    updated,
    normed, stage, gates, mask, left_w, right_w, means, scales,
    left_send, right_send, left_all, right_all, cross_send, cross_all,
    ls, lr, rs, rr, xs, xr, zs, zr,
):
    rows, cols, width = pair.shape
    half = width // 2
    mine = half // nc
    each = mine // parts
    tiles = tile_mask.shape[0]
    tile = rows * nr // tiles
    r = lax.axis_index("row")
    c = lax.axis_index("chan")

    barrier = pltpu.get_barrier_semaphore()

    @pl.loop(1, nc)
    def _(d):
        pl.semaphore_signal(
            barrier, inc=1, device_id={"chan": lax.rem(c + d, nc)}, device_id_type=MESH
        )

    @pl.when(r > 0)
    def _():
        pl.semaphore_signal(barrier, inc=1, device_id={"row": r - 1}, device_id_type=MESH)

    @pl.when(r < nr - 1)
    def _():
        pl.semaphore_signal(barrier, inc=1, device_id={"row": r + 1}, device_id_type=MESH)

    group = 8

    @pl.loop(0, rows // group)
    def _(g):
        v = pair[pl.ds(g * group, group)].astype(F32).reshape(group * cols, width)
        m = jnp.mean(v, axis=1, keepdims=True)
        s = jnp.mean(v * v, axis=1, keepdims=True)
        n = (v - m) * lax.rsqrt(s - m * m + epsilon) * in_gain[...] + in_shift[...]
        normed[pl.ds(pl.multiple_of(g * group * cols, group * cols), group * cols), :] = (
            n.astype(BF16).astype(F32)
        )

    tm = tile_mask[...].astype(F32)
    ids = lax.broadcasted_iota(jnp.int32, (cols, tiles), 0) + c * cols
    low = lax.broadcasted_iota(jnp.int32, (cols, tiles), 1) * tile
    col_hot = jnp.where((ids >= low) & (ids < low + tile), 1.0, 0.0)
    lane_t = lax.broadcasted_iota(jnp.int32, (tiles, width), 1)
    ids = jnp.where(lane_t < half, lane_t, lane_t - half) + r * rows
    low = lax.broadcasted_iota(jnp.int32, (tiles, width), 0) * tile
    row_hot = jnp.where((ids >= low) & (ids < low + tile), 1.0, 0.0)
    mask[...] = contract(contract(col_hot, tm, 1, 1), row_hot, 1, 0)

    def paired(w_ref):
        t = jnp.transpose(w_ref[...].astype(F32))
        return jnp.concatenate([t[:half], t[half:]], axis=1).astype(BF16)

    right_w[:half] = paired(right_gate)
    right_w[half:] = paired(right_proj)
    left_w[:half] = paired(left_gate)
    left_w[half:] = paired(left_proj)

    def at_column(k):
        return normed[pl.ds(k, rows, stride=cols), :].astype(BF16)

    def edges(w_ref, send):
        w = w_ref[...]
        empty = jnp.zeros((rows, width), BF16)

        @pl.loop(0, cols, unroll=4)
        def _(k):
            n = at_column(k)
            both = jnp.concatenate(
                [jnp.concatenate([n, empty], axis=1), jnp.concatenate([empty, n], axis=1)], axis=0
            )
            pre = contract(w, both, 1, 1)
            edge = mask[pl.ds(k, 1), :] * jax.nn.sigmoid(pre[:half]) * pre[half:]
            stage[pl.ds(k, half, stride=cols), :] = edge

        @pl.loop(0, half // group)
        def _(g):
            at = pl.ds(pl.multiple_of(g * group * cols, group * cols), group * cols)
            send[pl.ds(g * group, group)] = stage[at, :].astype(BF16).reshape(group, cols, width)

    def part_of(q):
        return pl.ds(q * each, each)

    def right_copy(d, q):
        to = lax.rem(c + d, nc)
        return pltpu.make_async_remote_copy(
            src_ref=right_send.at[pl.ds(to * mine + q * each, each)],
            dst_ref=right_all.at[r, part_of(q), pl.ds(pl.multiple_of(c * cols, cols), cols), :],
            send_sem=rs.at[d, q], recv_sem=rr.at[d, q],
            device_id={"chan": to}, device_id_type=MESH,
        )

    def left_copy(d, q):
        to = lax.rem(c + d, nc)
        return pltpu.make_async_remote_copy(
            src_ref=left_send.at[pl.ds(to * mine + q * each, each)],
            dst_ref=left_all.at[part_of(q), pl.ds(pl.multiple_of(c * cols, cols), cols), :],
            send_sem=ls.at[d, q], recv_sem=lr.at[d, q],
            device_id={"chan": to}, device_id_type=MESH,
        )

    def cross_copy(d, q):
        to = lax.rem(c + d, nc)
        return pltpu.make_async_remote_copy(
            src_ref=cross_send.at[part_of(q), pl.ds(pl.multiple_of(to * cols, cols), cols), :],
            dst_ref=cross_all.at[pl.ds(c * mine + q * each, each)],
            send_sem=xs.at[d, q], recv_sem=xr.at[d, q],
            device_id={"chan": to}, device_id_type=MESH,
        )

    def row_copy(block, q, way):
        return pltpu.make_async_remote_copy(
            src_ref=right_all.at[block, part_of(q)],
            dst_ref=right_all.at[block, part_of(q)],
            send_sem=zs.at[way, block, q], recv_sem=zr.at[block, q],
            device_id={"row": r + 1 - 2 * way}, device_id_type=MESH,
        )

    def each_peer(act):
        @pl.loop(1, nc)
        def _(d):
            act(d)

    own_cols = pl.ds(pl.multiple_of(c * cols, cols), cols)

    edges(right_w, right_send)
    pl.semaphore_wait(
        barrier, nc - 1 + jnp.where(r > 0, 1, 0) + jnp.where(r < nr - 1, 1, 0)
    )
    for q in range(parts):
        each_peer(lambda d: right_copy(d, q).start())
    right_all[r, :, own_cols, :] = right_send[pl.ds(c * mine, mine)]

    edges(left_w, left_send)
    for q in range(parts):
        each_peer(lambda d: left_copy(d, q).start())
    left_all[:, own_cols, :] = left_send[pl.ds(c * mine, mine)]

    lane = lax.broadcasted_iota(jnp.int32, (rows, width), 1)

    def products(q):
        each_peer(lambda d: left_copy(d, q).wait_recv())

        @pl.loop(0, nr)
        def _(b):
            for h in range(q * each, (q + 1) * each):
                both = contract(right_all[b, h], left_all[h], 0, 0)
                x = jnp.where(lane < half, both[:half], both[half:]).astype(BF16)
                cross_send[h, pl.ds(pl.multiple_of(b * rows, rows), rows), :] = x

        each_peer(lambda d: cross_copy(d, q).start())
        cross_all[pl.ds(c * mine + q * each, each)] = cross_send[part_of(q), own_cols, :]

    def pass_on(block, q, way, arrives):
        there = (block >= 0) & (block < nr)

        @pl.when(there)
        def _():
            if arrives:
                row_copy(block, q, way).wait_recv()

            @pl.when((r < nr - 1) if way == 0 else (r > 0))
            def _():
                row_copy(block, q, way).start()

    for t in range(parts + nr - 1):
        if t < parts:
            each_peer(lambda d: right_copy(d, t).wait_recv())
        for s in range(nr):
            q = t - s
            if 0 <= q < parts:
                pass_on(r - s, q, 0, s > 0)
                pass_on(r + s, q, 1, s > 0)
        if t == 0:
            @pl.loop(0, cols, unroll=4)
            def _(k):
                gates[k] = jax.nn.sigmoid(contract(at_column(k), out_gate[...], 1, 0))

        if t >= nr - 1:
            products(t - (nr - 1))

    for q in range(parts):
        each_peer(lambda d: cross_copy(d, q).wait_recv())

    def add_up(h, sums):
        x = cross_all[h].astype(F32)
        stage[pl.ds(pl.multiple_of(h * cols, cols), cols), :] = x
        return sums[0] + x, sums[1] + x * x

    zero = jnp.zeros((cols, width), F32)
    total, squares = lax.fori_loop(0, half, add_up, (zero, zero), unroll=4)
    total = total + pltpu.roll(total, half, 1)
    squares = squares + pltpu.roll(squares, half, 1)
    m = total / width
    means[...] = m
    scales[...] = lax.rsqrt(squares / width - m * m + epsilon)

    lane_h = lax.broadcasted_iota(jnp.int32, (half, width), 1)
    g = column(out_gain)
    s = column(out_shift)
    gain = jnp.where(lane_h < half, g[:half], g[half:])
    shift = jnp.where(lane_h < half, s[:half], s[half:])
    w_out = jnp.concatenate([out_proj[:half], out_proj[half:]], axis=1)

    @pl.loop(0, cols, unroll=4)
    def _(j):
        x = stage[pl.ds(j, half, stride=cols), :]
        x = (x - means[pl.ds(j, 1), :]) * scales[pl.ds(j, 1), :] * gain + shift
        y = contract(x.astype(BF16), w_out, 0, 0)
        normed[pl.ds(j, rows, stride=cols), :] = gates[j] * (y[:half, :width] + y[half:, width:])

    @pl.loop(0, rows // group)
    def _(g):
        at = pl.ds(pl.multiple_of(g * group * cols, group * cols), group * cols)
        updated[pl.ds(g * group, group)] = normed[at, :].astype(BF16).reshape(group, cols, width)

    for q in range(parts):
        def sent(d):
            right_copy(d, q).wait_send()
            left_copy(d, q).wait_send()
            cross_copy(d, q).wait_send()

        each_peer(sent)

    @pl.loop(0, nr)
    def _(block):
        for q in range(parts):
            @pl.when((block <= r) & (r < nr - 1))
            def _():
                row_copy(block, q, 0).wait_send()

            @pl.when((block >= r) & (r > 0))
            def _():
                row_copy(block, q, 1).wait_send()


def local(nr, nc, pair, tile_mask, in_gain, in_shift, left_gate, left_proj, right_gate, right_proj,
          out_gain, out_shift, out_gate, out_proj):
    rows, cols, width = pair.shape
    half = width // 2
    assert rows == half
    mine = half // nc
    parts = math.gcd(mine, 4)
    total = cols * nc
    dma = pltpu.SemaphoreType.DMA
    vmem = pltpu.VMEM
    return pl.pallas_call(
        functools.partial(kernel, nr, nc, parts),
        out_shape=jax.ShapeDtypeStruct(pair.shape, BF16),
        in_specs=[pl.BlockSpec(memory_space=pltpu.VMEM)] * 12,
        out_specs=pl.BlockSpec(memory_space=pltpu.VMEM),
        scratch_shapes=[
            vmem((rows * cols, width), F32),
            vmem((half * cols, width), F32),
            vmem((cols, rows, width), F32),
            vmem((cols, width), F32),
            vmem((width, 2 * width), BF16),
            vmem((width, 2 * width), BF16),
            vmem((cols, width), F32),
            vmem((cols, width), F32),
            vmem((half, cols, width), BF16),
            vmem((half, cols, width), BF16),
            vmem((mine, total, width), BF16),
            vmem((nr, mine, total, width), BF16),
            vmem((mine, rows * nr, width), BF16),
            vmem((half, cols, width), BF16),
            dma((nc, parts)), dma((nc, parts)),
            dma((nc, parts)), dma((nc, parts)),
            dma((nc, parts)), dma((nc, parts)),
            dma((2, nr, parts)), dma((nr, parts)),
        ],
        compiler_params=pltpu.CompilerParams(
            collective_id=0, has_side_effects=True, vmem_limit_bytes=48 * 1024 * 1024
        ),
    )(
        pair, tile_mask, in_gain[None], in_shift[None], left_gate, left_proj, right_gate,
        right_proj, out_gain[None], out_shift[None], out_gate, out_proj,
    )


def solution(mesh):
    placed = (P("row", "chan", None), P(), P(), P(), P(), P(), P(), P(), P(), P(), P(), P())
    return jax.shard_map(
        functools.partial(local, mesh.shape["row"], mesh.shape["chan"]),
        mesh=mesh, in_specs=placed, out_specs=P("row", "chan", None), check_vma=False,
    )
```

```python
import functools
import math

import jax
import jax.numpy as jnp
from jax import lax
from jax.experimental import pallas as pl
from jax.experimental.pallas import tpu as pltpu
from jax.sharding import PartitionSpec as P

MESH = pl.DeviceIdType.MESH
F32 = jnp.float32
BF16 = jnp.bfloat16
epsilon = 1e-05


def contract(a, b, da, db):
    return lax.dot_general(a, b, (((da,), (db,)), ((), ())), preferred_element_type=F32)


def column(row_ref):
    width = row_ref.shape[1]
    return jnp.transpose(jnp.broadcast_to(row_ref[...], (width, width)))


def kernel(
    nr, nc, parts,
    *refs,
):
    operands, (updated,), held, rest = refs[:12], refs[12:13], refs[13:25], refs[25:]
    body(nr, nc, parts, operands, held, updated, *rest)


def body(
    nr, nc, parts, operands, held, updated,
    fetched, normed, stage, gates, mask, left_w, right_w, means, scales,
    left_send, right_send, left_all, right_all, cross_send, cross_all,
    left_far, far_send,
    ls, lr, rs, rr, xs, xr, zs, zr, fs, fr, gs, gr,
):
    fetches = [
        pltpu.make_async_copy(source, target, fetched.at[n])
        for n, (source, target) in enumerate(zip(operands, held))
    ]
    for fetch in fetches:
        fetch.start()
    (pair, tile_mask, in_gain, in_shift, left_gate, left_proj, right_gate, right_proj,
     out_gain, out_shift, out_gate, out_proj) = held
    rows, cols, width = pair.shape
    half = width // 2
    mine = half // nc
    each = mine // parts
    tiles = tile_mask.shape[0]
    tile = rows * nr // tiles
    r = lax.axis_index("row")
    c = lax.axis_index("chan")

    barrier = pltpu.get_barrier_semaphore()

    @pl.loop(1, nc)
    def _(d):
        pl.semaphore_signal(
            barrier, inc=1, device_id={"chan": lax.rem(c + d, nc)}, device_id_type=MESH
        )

    @pl.when(r > 0)
    def _():
        pl.semaphore_signal(barrier, inc=1, device_id={"row": r - 1}, device_id_type=MESH)

    @pl.when(r < nr - 1)
    def _():
        pl.semaphore_signal(barrier, inc=1, device_id={"row": r + 1}, device_id_type=MESH)

    for n in (0, 2, 3):
        fetches[n].wait()

    group = 8

    @pl.loop(0, rows // group)
    def _(g):
        v = pair[pl.ds(g * group, group)].astype(F32).reshape(group * cols, width)
        m = jnp.mean(v, axis=1, keepdims=True)
        s = jnp.mean(v * v, axis=1, keepdims=True)
        n = (v - m) * lax.rsqrt(s - m * m + epsilon) * in_gain[...] + in_shift[...]
        normed[pl.ds(pl.multiple_of(g * group * cols, group * cols), group * cols), :] = (
            n.astype(BF16).astype(F32)
        )

    for n in (1, 4, 5, 6, 7, 8, 9, 10, 11):
        fetches[n].wait()

    tm = tile_mask[...].astype(F32)
    ids = lax.broadcasted_iota(jnp.int32, (cols, tiles), 0) + c * cols
    low = lax.broadcasted_iota(jnp.int32, (cols, tiles), 1) * tile
    col_hot = jnp.where((ids >= low) & (ids < low + tile), 1.0, 0.0)
    lane_t = lax.broadcasted_iota(jnp.int32, (tiles, width), 1)
    ids = jnp.where(lane_t < half, lane_t, lane_t - half) + r * rows
    low = lax.broadcasted_iota(jnp.int32, (tiles, width), 0) * tile
    row_hot = jnp.where((ids >= low) & (ids < low + tile), 1.0, 0.0)
    mask[...] = contract(contract(col_hot, tm, 1, 1), row_hot, 1, 0)

    def paired(w_ref):
        t = jnp.transpose(w_ref[...].astype(F32))
        return jnp.concatenate([t[:half], t[half:]], axis=1).astype(BF16)

    right_w[:half] = paired(right_gate)
    right_w[half:] = paired(right_proj)
    left_w[:half] = paired(left_gate)
    left_w[half:] = paired(left_proj)

    def at_column(k):
        return normed[pl.ds(k, rows, stride=cols), :].astype(BF16)

    def edges(w_ref, send):
        w = w_ref[...]
        empty = jnp.zeros((rows, width), BF16)

        @pl.loop(0, cols, unroll=4)
        def _(k):
            n = at_column(k)
            both = jnp.concatenate(
                [jnp.concatenate([n, empty], axis=1), jnp.concatenate([empty, n], axis=1)], axis=0
            )
            pre = contract(w, both, 1, 1)
            edge = mask[pl.ds(k, 1), :] * jax.nn.sigmoid(pre[:half]) * pre[half:]
            stage[pl.ds(k, half, stride=cols), :] = edge

        @pl.loop(0, half // group)
        def _(g):
            at = pl.ds(pl.multiple_of(g * group * cols, group * cols), group * cols)
            send[pl.ds(g * group, group)] = stage[at, :].astype(BF16).reshape(group, cols, width)

    def part_of(q):
        return pl.ds(q * each, each)

    def right_copy(d, q):
        to = lax.rem(c + d, nc)
        return pltpu.make_async_remote_copy(
            src_ref=right_send.at[pl.ds(to * mine + q * each, each)],
            dst_ref=right_all.at[r, part_of(q), pl.ds(pl.multiple_of(c * cols, cols), cols), :],
            send_sem=rs.at[d, q], recv_sem=rr.at[d, q],
            device_id={"chan": to}, device_id_type=MESH,
        )

    def left_copy(d, q):
        to = lax.rem(c + d, nc)
        return pltpu.make_async_remote_copy(
            src_ref=left_send.at[pl.ds(to * mine + q * each, each)],
            dst_ref=left_all.at[part_of(q), pl.ds(pl.multiple_of(c * cols, cols), cols), :],
            send_sem=ls.at[d, q], recv_sem=lr.at[d, q],
            device_id={"chan": to}, device_id_type=MESH,
        )

    def cross_copy(d, q):
        to = lax.rem(c + d, nc)
        return pltpu.make_async_remote_copy(
            src_ref=cross_send.at[part_of(q), pl.ds(pl.multiple_of(to * cols, cols), cols), :],
            dst_ref=cross_all.at[pl.ds(c * mine + q * each, each)],
            send_sem=xs.at[d, q], recv_sem=xr.at[d, q],
            device_id={"chan": to}, device_id_type=MESH,
        )

    def row_copy(block, q, way):
        return pltpu.make_async_remote_copy(
            src_ref=right_all.at[block, part_of(q)],
            dst_ref=right_all.at[block, part_of(q)],
            send_sem=zs.at[way, block, q], recv_sem=zr.at[block, q],
            device_id={"row": r + 1 - 2 * way}, device_id_type=MESH,
        )

    def each_peer(act):
        @pl.loop(1, nc)
        def _(d):
            act(d)

    own_cols = pl.ds(pl.multiple_of(c * cols, cols), cols)

    edges(right_w, right_send)
    pl.semaphore_wait(
        barrier, nc - 1 + jnp.where(r > 0, 1, 0) + jnp.where(r < nr - 1, 1, 0)
    )
    for q in range(parts):
        each_peer(lambda d: right_copy(d, q).start())
    right_all[r, :, own_cols, :] = right_send[pl.ds(c * mine, mine)]

    edges(left_w, left_send)
    for q in range(parts):
        each_peer(lambda d: left_copy(d, q).start())
    left_all[:, own_cols, :] = left_send[pl.ds(c * mine, mine)]

    lane = lax.broadcasted_iota(jnp.int32, (rows, width), 1)

    first, last = r == 0, r == nr - 1
    share = nr // 2
    low_part, high_part = pl.ds(0, share * rows), pl.ds(share * rows, (nr - share) * rows)

    def left_over(q, way):
        return pltpu.make_async_remote_copy(
            src_ref=left_all.at[part_of(q)], dst_ref=left_far.at[part_of(q)],
            send_sem=fs.at[q], recv_sem=fr.at[q],
            device_id={"row": r + 1 - 2 * way}, device_id_type=MESH,
        )

    def products_over(q, way):
        there = high_part if way else low_part
        return pltpu.make_async_remote_copy(
            src_ref=far_send.at[part_of(q), there], dst_ref=cross_send.at[part_of(q), there],
            send_sem=gs.at[q], recv_sem=gr.at[q],
            device_id={"row": r + 1 - 2 * way}, device_id_type=MESH,
        )

    def multiply(q, start, stop, left, into):
        @pl.loop(start, stop)
        def _(b):
            for h in range(q * each, (q + 1) * each):
                both = contract(right_all[b, h], left[h], 0, 0)
                x = jnp.where(lane < half, both[:half], both[half:]).astype(BF16)
                into[h, pl.ds(pl.multiple_of(b * rows, rows), rows), :] = x

    def send_products(q):
        each_peer(lambda d: cross_copy(d, q).start())
        cross_all[pl.ds(c * mine + q * each, each)] = cross_send[part_of(q), own_cols, :]

    def own_products(q):
        @pl.when(first)
        def _():
            multiply(q, 0, share, left_all, cross_send)

        @pl.when(last)
        def _():
            multiply(q, share, nr, left_all, cross_send)

        @pl.when(jnp.logical_not(first | last))
        def _():
            each_peer(lambda d: left_copy(d, q).wait_recv())
            multiply(q, 0, nr, left_all, cross_send)
            send_products(q)

    def far_products(q):
        @pl.when(r == 1)
        def _():
            left_over(q, 0).wait_recv()
            multiply(q, share, nr, left_far, far_send)
            products_over(q, 1).start()

        @pl.when(r == nr - 2)
        def _():
            left_over(q, 1).wait_recv()
            multiply(q, 0, share, left_far, far_send)
            products_over(q, 0).start()

        @pl.when(first)
        def _():
            products_over(q, 1).wait_recv()
            send_products(q)

        @pl.when(last)
        def _():
            products_over(q, 0).wait_recv()
            send_products(q)

    def pass_on(block, q, way, arrives):
        if way == 0:
            there = (block >= 0) & jnp.logical_not(last & (block < share))
            goes = (r < nr - 2) | ((r == nr - 2) & (block >= share))
        else:
            there = (block < nr) & jnp.logical_not(first & (block >= share))
            goes = (r > 1) | ((r == 1) & (block < share))

        @pl.when(there)
        def _():
            if arrives:
                row_copy(block, q, way).wait_recv()

            @pl.when(goes)
            def _():
                row_copy(block, q, way).start()

    @pl.when(first | last)
    def _():
        def right_on(q):
            each_peer(lambda d: right_copy(d, q).wait_recv())

            @pl.when(first)
            def _():
                row_copy(r, q, 0).start()

            @pl.when(last)
            def _():
                row_copy(r, q, 1).start()

        def left_on(q):
            each_peer(lambda d: left_copy(d, q).wait_recv())

            @pl.when(first)
            def _():
                left_over(q, 0).start()

            @pl.when(last)
            def _():
                left_over(q, 1).start()

        for q in range(parts + 1):
            if q < parts:
                right_on(q)
            if q > 0:
                left_on(q - 1)

    for t in range(parts + nr - 1):
        if t < parts:
            @pl.when(jnp.logical_not(first | last))
            def _():
                each_peer(lambda d: right_copy(d, t).wait_recv())
                pass_on(r, t, 0, False)
                pass_on(r, t, 1, False)
        for s in range(1, nr - 1):
            q = t - s
            if 0 <= q < parts:
                pass_on(r - s, q, 0, True)
                pass_on(r + s, q, 1, True)
        if t == 0:
            @pl.loop(0, cols, unroll=4)
            def _(k):
                gates[k] = jax.nn.sigmoid(contract(at_column(k), out_gate[...], 1, 0))

        if 0 <= t - (nr - 2) < parts:
            own_products(t - (nr - 2))
        if t >= nr - 1:
            far_products(t - (nr - 1))

    for q in range(parts):
        each_peer(lambda d: cross_copy(d, q).wait_recv())

    def add_up(h, sums):
        x = cross_all[h].astype(F32)
        stage[pl.ds(pl.multiple_of(h * cols, cols), cols), :] = x
        return sums[0] + x, sums[1] + x * x

    zero = jnp.zeros((cols, width), F32)
    total, squares = lax.fori_loop(0, half, add_up, (zero, zero), unroll=4)
    total = total + pltpu.roll(total, half, 1)
    squares = squares + pltpu.roll(squares, half, 1)
    m = total / width
    means[...] = m
    scales[...] = lax.rsqrt(squares / width - m * m + epsilon)

    lane_h = lax.broadcasted_iota(jnp.int32, (half, width), 1)
    g = column(out_gain)
    s = column(out_shift)
    gain = jnp.where(lane_h < half, g[:half], g[half:])
    shift = jnp.where(lane_h < half, s[:half], s[half:])
    w_out = jnp.concatenate([out_proj[:half], out_proj[half:]], axis=1)

    @pl.loop(0, cols, unroll=4)
    def _(j):
        x = stage[pl.ds(j, half, stride=cols), :]
        x = (x - means[pl.ds(j, 1), :]) * scales[pl.ds(j, 1), :] * gain + shift
        y = contract(x.astype(BF16), w_out, 0, 0)
        normed[pl.ds(j, rows, stride=cols), :] = gates[j] * (y[:half, :width] + y[half:, width:])

    @pl.loop(0, rows // group)
    def _(g):
        at = pl.ds(pl.multiple_of(g * group * cols, group * cols), group * cols)
        updated[pl.ds(g * group, group)] = normed[at, :].astype(BF16).reshape(group, cols, width)

    for q in range(parts):
        def sent(d):
            right_copy(d, q).wait_send()
            left_copy(d, q).wait_send()
            cross_copy(d, q).wait_send()

        each_peer(sent)

    for q in range(parts):
        @pl.when(first | last)
        def _():
            left_over(q, 0).wait_send()

        @pl.when((r == 1) | (r == nr - 2))
        def _():
            products_over(q, 0).wait_send()

        @pl.loop(0, nr)
        def _(block):
            @pl.when((block <= r) & ((r < nr - 2) | ((r == nr - 2) & (block >= share))))
            def _():
                row_copy(block, q, 0).wait_send()

            @pl.when((block >= r) & ((r > 1) | ((r == 1) & (block < share))))
            def _():
                row_copy(block, q, 1).wait_send()


def local(nr, nc, pair, tile_mask, in_gain, in_shift, left_gate, left_proj, right_gate, right_proj,
          out_gain, out_shift, out_gate, out_proj):
    rows, cols, width = pair.shape
    half = width // 2
    assert rows == half and nr >= 4 and nr % 2 == 0
    mine = half // nc
    parts = math.gcd(mine, 4)
    total = cols * nc
    dma = pltpu.SemaphoreType.DMA
    vmem = pltpu.VMEM
    operands = (
        pair, tile_mask, in_gain[None], in_shift[None], left_gate, left_proj, right_gate,
        right_proj, out_gain[None], out_shift[None], out_gate, out_proj,
    )
    return pl.pallas_call(
        functools.partial(kernel, nr, nc, parts),
        out_shape=jax.ShapeDtypeStruct(pair.shape, BF16),
        in_specs=[pl.BlockSpec(memory_space=pl.ANY)] * 12,
        out_specs=pl.BlockSpec(memory_space=pltpu.VMEM),
        scratch_shapes=[vmem(a.shape, a.dtype) for a in operands] + [
            dma((len(operands),)),
            vmem((rows * cols, width), F32),
            vmem((half * cols, width), F32),
            vmem((cols, rows, width), F32),
            vmem((cols, width), F32),
            vmem((width, 2 * width), BF16),
            vmem((width, 2 * width), BF16),
            vmem((cols, width), F32),
            vmem((cols, width), F32),
            vmem((half, cols, width), BF16),
            vmem((half, cols, width), BF16),
            vmem((mine, total, width), BF16),
            vmem((nr, mine, total, width), BF16),
            vmem((mine, rows * nr, width), BF16),
            vmem((half, cols, width), BF16),
            vmem((mine, total, width), BF16),
            vmem((mine, rows * nr, width), BF16),
            dma((nc, parts)), dma((nc, parts)),
            dma((nc, parts)), dma((nc, parts)),
            dma((nc, parts)), dma((nc, parts)),
            dma((2, nr, parts)), dma((nr, parts)),
            dma((parts,)), dma((parts,)), dma((parts,)), dma((parts,)),
        ],
        compiler_params=pltpu.CompilerParams(
            collective_id=0, has_side_effects=True, vmem_limit_bytes=60 * 1024 * 1024
        ),
    )(*operands)


def solution(mesh):
    placed = (P("row", "chan", None), P(), P(), P(), P(), P(), P(), P(), P(), P(), P(), P())
    return jax.shard_map(
        functools.partial(local, mesh.shape["row"], mesh.shape["chan"]),
        mesh=mesh, in_specs=placed, out_specs=P("row", "chan", None), check_vma=False,
    )
```

```python
import functools
import math

import jax
import jax.numpy as jnp
from jax import lax
from jax.experimental import pallas as pl
from jax.experimental.pallas import tpu as pltpu
from jax.sharding import PartitionSpec as P

MESH = pl.DeviceIdType.MESH
F32 = jnp.float32
BF16 = jnp.bfloat16
epsilon = 1e-05


def contract(a, b, da, db):
    return lax.dot_general(a, b, (((da,), (db,)), ((), ())), preferred_element_type=F32)


def column(row_ref):
    width = row_ref.shape[1]
    return jnp.transpose(jnp.broadcast_to(row_ref[...], (width, width)))


def kernel(
    nr, nc, parts,
    *refs,
):
    operands, (updated,), held, rest = refs[:12], refs[12:13], refs[13:25], refs[25:]
    body(nr, nc, parts, operands, held, updated, *rest)


def body(
    nr, nc, parts, operands, held, updated,
    fetched, normed, stage, gates, mask, left_w, right_w, means, scales, gain, shift, out_w,
    left_send, right_send, left_all, right_all, cross_send, cross_all,
    left_far, far_send,
    ls, lr, rs, rr, xs, xr, zs, zr, fs, fr, gs,
):
    fetches = [
        pltpu.make_async_copy(source, target, fetched.at[n])
        for n, (source, target) in enumerate(zip(operands, held))
    ]
    for fetch in fetches:
        fetch.start()
    (pair, tile_mask, in_gain, in_shift, left_gate, left_proj, right_gate, right_proj,
     out_gain, out_shift, out_gate, out_proj) = held
    rows, cols, width = pair.shape
    half = width // 2
    mine = half // nc
    each = mine // parts
    tiles = tile_mask.shape[0]
    tile = rows * nr // tiles
    r = lax.axis_index("row")
    c = lax.axis_index("chan")

    first, last = r == 0, r == nr - 1
    inner = jnp.logical_not(first | last)
    share, split = nr // 2, nc // 2

    barrier = pltpu.get_barrier_semaphore()

    @pl.loop(1, nc)
    def _(d):
        pl.semaphore_signal(
            barrier, inc=1, device_id={"chan": lax.rem(c + d, nc)}, device_id_type=MESH
        )

    @pl.when(r > 0)
    def _():
        pl.semaphore_signal(barrier, inc=1, device_id={"row": r - 1}, device_id_type=MESH)

    @pl.when(r < nr - 1)
    def _():
        pl.semaphore_signal(barrier, inc=1, device_id={"row": r + 1}, device_id_type=MESH)

    def greet(row):
        @pl.loop(1, nc)
        def _(d):
            pl.semaphore_signal(
                barrier, inc=1, device_id={"row": row, "chan": lax.rem(c + d, nc)},
                device_id_type=MESH,
            )

    @pl.when(last & (c < split))
    def _():
        greet(r - 1)

    @pl.when(first & (c >= split))
    def _():
        greet(r + 1)

    for n in (0, 2, 3):
        fetches[n].wait()

    group = 8

    @pl.loop(0, rows // group, unroll=2)
    def _(g):
        v = pair[pl.ds(g * group, group)].astype(F32).reshape(group * cols, width)
        m = jnp.mean(v, axis=1, keepdims=True)
        s = jnp.mean(v * v, axis=1, keepdims=True)
        n = (v - m) * lax.rsqrt(s - m * m + epsilon) * in_gain[...] + in_shift[...]
        normed[pl.ds(pl.multiple_of(g * group * cols, group * cols), group * cols), :] = (
            n.astype(BF16).astype(F32)
        )

    for n in (1, 4, 5, 6, 7, 8, 9, 10, 11):
        fetches[n].wait()

    tm = tile_mask[...].astype(F32)
    ids = lax.broadcasted_iota(jnp.int32, (cols, tiles), 0) + c * cols
    low = lax.broadcasted_iota(jnp.int32, (cols, tiles), 1) * tile
    col_hot = jnp.where((ids >= low) & (ids < low + tile), 1.0, 0.0)
    lane_t = lax.broadcasted_iota(jnp.int32, (tiles, width), 1)
    ids = jnp.where(lane_t < half, lane_t, lane_t - half) + r * rows
    low = lax.broadcasted_iota(jnp.int32, (tiles, width), 0) * tile
    row_hot = jnp.where((ids >= low) & (ids < low + tile), 1.0, 0.0)
    mask[...] = contract(contract(col_hot, tm, 1, 1), row_hot, 1, 0)

    def paired(w_ref):
        t = jnp.transpose(w_ref[...].astype(F32))
        return jnp.concatenate([t[:half], t[half:]], axis=1).astype(BF16)

    right_w[:half] = paired(right_gate)
    right_w[half:] = paired(right_proj)
    left_w[:half] = paired(left_gate)
    left_w[half:] = paired(left_proj)

    def at_column(k):
        return normed[pl.ds(k, rows, stride=cols), :].astype(BF16)

    def edges(w_ref, send):
        w = w_ref[...]
        empty = jnp.zeros((rows, width), BF16)

        @pl.loop(0, cols, unroll=4)
        def _(k):
            n = at_column(k)
            both = jnp.concatenate(
                [jnp.concatenate([n, empty], axis=1), jnp.concatenate([empty, n], axis=1)], axis=0
            )
            pre = contract(w, both, 1, 1)
            edge = mask[pl.ds(k, 1), :] * jax.nn.sigmoid(pre[:half]) * pre[half:]
            stage[pl.ds(k, half, stride=cols), :] = edge

        @pl.loop(0, half // group)
        def _(g):
            at = pl.ds(pl.multiple_of(g * group * cols, group * cols), group * cols)
            send[pl.ds(g * group, group)] = stage[at, :].astype(BF16).reshape(group, cols, width)

    def part_of(q):
        return pl.ds(q * each, each)

    def right_copy(d, q):
        to = lax.rem(c + d, nc)
        return pltpu.make_async_remote_copy(
            src_ref=right_send.at[pl.ds(to * mine + q * each, each)],
            dst_ref=right_all.at[r, part_of(q), pl.ds(pl.multiple_of(c * cols, cols), cols), :],
            send_sem=rs.at[d, q], recv_sem=rr.at[d, q],
            device_id={"chan": to}, device_id_type=MESH,
        )

    def left_copy(d, q):
        to = lax.rem(c + d, nc)
        return pltpu.make_async_remote_copy(
            src_ref=left_send.at[pl.ds(to * mine + q * each, each)],
            dst_ref=left_all.at[part_of(q), pl.ds(pl.multiple_of(c * cols, cols), cols), :],
            send_sem=ls.at[d, q], recv_sem=lr.at[d, q],
            device_id={"chan": to}, device_id_type=MESH,
        )

    def cross_copy(d, q):
        to = lax.rem(c + d, nc)
        return pltpu.make_async_remote_copy(
            src_ref=cross_send.at[part_of(q), pl.ds(pl.multiple_of(to * cols, cols), cols), :],
            dst_ref=cross_all.at[pl.ds(c * mine + q * each, each)],
            send_sem=xs.at[d, q], recv_sem=xr.at[d, q],
            device_id={"chan": to}, device_id_type=MESH,
        )

    def row_copy(block, q, way):
        return pltpu.make_async_remote_copy(
            src_ref=right_all.at[block, part_of(q)],
            dst_ref=right_all.at[block, part_of(q)],
            send_sem=zs.at[way, block, q], recv_sem=zr.at[block, q],
            device_id={"row": r + 1 - 2 * way}, device_id_type=MESH,
        )

    def each_peer(act):
        @pl.loop(1, nc)
        def _(d):
            act(d)

    own_cols = pl.ds(pl.multiple_of(c * cols, cols), cols)

    edges(right_w, right_send)
    pl.semaphore_wait(
        barrier,
        nc - 1 + jnp.where(r > 0, 1, 0) + jnp.where(r < nr - 1, 1, 0)
        + jnp.where(r == nr - 2, split - jnp.where(c < split, 1, 0), 0)
        + jnp.where(r == 1, nc - split - jnp.where(c >= split, 1, 0), 0),
    )
    for q in range(parts):
        each_peer(lambda d: right_copy(d, q).start())
    right_all[r, :, own_cols, :] = right_send[pl.ds(c * mine, mine)]

    lane = lax.broadcasted_iota(jnp.int32, (rows, width), 1)

    def left_over(q, way):
        return pltpu.make_async_remote_copy(
            src_ref=left_all.at[part_of(q)], dst_ref=left_far.at[part_of(q)],
            send_sem=fs.at[q], recv_sem=fr.at[q],
            device_id={"row": r + 1 - 2 * way}, device_id_type=MESH,
        )

    def far_copy(d, q, way):
        to = lax.rem(c + d, nc)
        return pltpu.make_async_remote_copy(
            src_ref=far_send.at[part_of(q), pl.ds(pl.multiple_of(to * cols, cols), cols), :],
            dst_ref=cross_all.at[pl.ds(c * mine + q * each, each)],
            send_sem=gs.at[d, q], recv_sem=xr.at[d, q],
            device_id={"row": r + 1 - 2 * way, "chan": to}, device_id_type=MESH,
        )

    def each_far(way, act):
        @pl.loop(0, nc)
        def _(d):
            to = lax.rem(c + d, nc)

            @pl.when((to >= split) if way else (to < split))
            def _():
                act(d)

    def is_near(to):
        return inner | (last & (to >= split)) | (first & (to < split))

    def each_near(act):
        @pl.loop(1, nc)
        def _(d):
            @pl.when(is_near(lax.rem(c + d, nc)))
            def _():
                act(d)

    def multiply(q, start, stop, left, into):
        @pl.loop(start, stop, unroll=2)
        def _(b):
            for h in range(q * each, (q + 1) * each):
                both = contract(right_all[b, h], left[h], 0, 0)
                x = jnp.where(lane < half, both[:half], both[half:]).astype(BF16)
                into[h, pl.ds(pl.multiple_of(b * rows, rows), rows), :] = x

    def own_products(q):
        @pl.when(first)
        def _():
            multiply(q, 0, share, left_all, cross_send)

        @pl.when(last)
        def _():
            multiply(q, share, nr, left_all, cross_send)

        @pl.when(inner)
        def _():
            each_peer(lambda d: left_copy(d, q).wait_recv())
            multiply(q, 0, nr, left_all, cross_send)

        each_near(lambda d: cross_copy(d, q).start())

        @pl.when(is_near(c))
        def _():
            cross_all[pl.ds(c * mine + q * each, each)] = cross_send[part_of(q), own_cols, :]

    def far_products(q):
        @pl.when(r == 1)
        def _():
            left_over(q, 0).wait_recv()
            multiply(q, share, nr, left_far, far_send)
            each_far(1, lambda d: far_copy(d, q, 1).start())

        @pl.when(r == nr - 2)
        def _():
            left_over(q, 1).wait_recv()
            multiply(q, 0, share, left_far, far_send)
            each_far(0, lambda d: far_copy(d, q, 0).start())

    def pass_on(block, q, way, arrives):
        if way == 0:
            there = (block >= 0) & jnp.logical_not(last & (block < share))
            goes = (r < nr - 2) | ((r == nr - 2) & (block >= share))
        else:
            there = (block < nr) & jnp.logical_not(first & (block >= share))
            goes = (r > 1) | ((r == 1) & (block < share))

        @pl.when(there)
        def _():
            if arrives:
                row_copy(block, q, way).wait_recv()

            @pl.when(goes)
            def _():
                row_copy(block, q, way).start()

    def own_on(q):
        each_peer(lambda d: right_copy(d, q).wait_recv())
        pass_on(r, q, 0, False)
        pass_on(r, q, 1, False)

    @pl.loop(0, cols, unroll=4)
    def _(k):
        gates[k] = jax.nn.sigmoid(contract(at_column(k), out_gate[...], 1, 0))

    own_on(0)

    edges(left_w, left_send)
    for q in range(parts):
        each_peer(lambda d: left_copy(d, q).start())
    left_all[:, own_cols, :] = left_send[pl.ds(c * mine, mine)]

    lane_h = lax.broadcasted_iota(jnp.int32, (half, width), 1)
    g = column(out_gain)
    s = column(out_shift)
    gain[...] = jnp.where(lane_h < half, g[:half], g[half:])
    shift[...] = jnp.where(lane_h < half, s[:half], s[half:])
    out_w[...] = jnp.concatenate([out_proj[:half], out_proj[half:]], axis=1)

    @pl.when(first | last)
    def _():
        def left_on(q):
            each_peer(lambda d: left_copy(d, q).wait_recv())

            @pl.when(first)
            def _():
                left_over(q, 0).start()

            @pl.when(last)
            def _():
                left_over(q, 1).start()

        for q in range(1, parts):
            own_on(q)
            left_on(q - 1)
        left_on(parts - 1)

    for t in range(parts + nr - 1):
        if 0 < t < parts:
            @pl.when(inner)
            def _():
                own_on(t)
        for s in range(1, nr - 1):
            q = t - s
            if 0 <= q < parts:
                pass_on(r - s, q, 0, True)
                pass_on(r + s, q, 1, True)
        if 0 <= t - (nr - 2) < parts:
            own_products(t - (nr - 2))
        if t >= nr - 1:
            far_products(t - (nr - 1))

    total = jnp.zeros((cols, width), F32)
    squares = total
    for q in range(parts):
        each_peer(lambda d: cross_copy(d, q).wait_recv())

        @pl.when(first & (c >= split))
        def _():
            far_copy(0, q, 0).wait_recv()

        @pl.when(last & (c < split))
        def _():
            far_copy(0, q, 1).wait_recv()

        def add_up(p, sums):
            for e in range(each):
                h = p * mine + q * each + e
                x = cross_all[h].astype(F32)
                stage[pl.ds(pl.multiple_of(h * cols, cols), cols), :] = x
                sums = sums[0] + x, sums[1] + x * x
            return sums

        total, squares = lax.fori_loop(0, nc, add_up, (total, squares), unroll=4)

    total = total + pltpu.roll(total, half, 1)
    squares = squares + pltpu.roll(squares, half, 1)
    m = total / width
    means[...] = m
    scales[...] = lax.rsqrt(squares / width - m * m + epsilon)

    @pl.loop(0, cols, unroll=4)
    def _(j):
        x = stage[pl.ds(j, half, stride=cols), :]
        x = (x - means[pl.ds(j, 1), :]) * scales[pl.ds(j, 1), :] * gain[...] + shift[...]
        y = contract(x.astype(BF16), out_w[...], 0, 0)
        normed[pl.ds(j, rows, stride=cols), :] = gates[j] * (y[:half, :width] + y[half:, width:])

    @pl.loop(0, rows // group)
    def _(g):
        at = pl.ds(pl.multiple_of(g * group * cols, group * cols), group * cols)
        updated[pl.ds(g * group, group)] = normed[at, :].astype(BF16).reshape(group, cols, width)

    for q in range(parts):
        def sent(d):
            right_copy(d, q).wait_send()
            left_copy(d, q).wait_send()

        each_peer(sent)
        each_near(lambda d: cross_copy(d, q).wait_send())

        @pl.when(r == 1)
        def _():
            each_far(1, lambda d: far_copy(d, q, 1).wait_send())

        @pl.when(r == nr - 2)
        def _():
            each_far(0, lambda d: far_copy(d, q, 0).wait_send())

    for q in range(parts):
        @pl.when(first | last)
        def _():
            left_over(q, 0).wait_send()

        @pl.loop(0, nr)
        def _(block):
            @pl.when((block <= r) & ((r < nr - 2) | ((r == nr - 2) & (block >= share))))
            def _():
                row_copy(block, q, 0).wait_send()

            @pl.when((block >= r) & ((r > 1) | ((r == 1) & (block < share))))
            def _():
                row_copy(block, q, 1).wait_send()


def local(nr, nc, pair, tile_mask, in_gain, in_shift, left_gate, left_proj, right_gate, right_proj,
          out_gain, out_shift, out_gate, out_proj):
    rows, cols, width = pair.shape
    half = width // 2
    assert rows == half and nr >= 4 and nr % 2 == 0 and nc % 2 == 0
    mine = half // nc
    parts = math.gcd(mine, 4)
    total = cols * nc
    dma = pltpu.SemaphoreType.DMA
    vmem = pltpu.VMEM
    operands = (
        pair, tile_mask, in_gain[None], in_shift[None], left_gate, left_proj, right_gate,
        right_proj, out_gain[None], out_shift[None], out_gate, out_proj,
    )
    return pl.pallas_call(
        functools.partial(kernel, nr, nc, parts),
        out_shape=jax.ShapeDtypeStruct(pair.shape, BF16),
        in_specs=[pl.BlockSpec(memory_space=pltpu.HBM)] * 12,
        out_specs=pl.BlockSpec(memory_space=pltpu.VMEM),
        scratch_shapes=[vmem(a.shape, a.dtype) for a in operands] + [
            dma((len(operands),)),
            vmem((rows * cols, width), F32),
            vmem((half * cols, width), F32),
            vmem((cols, rows, width), F32),
            vmem((cols, width), F32),
            vmem((width, 2 * width), BF16),
            vmem((width, 2 * width), BF16),
            vmem((cols, width), F32),
            vmem((cols, width), F32),
            vmem((half, width), F32),
            vmem((half, width), F32),
            vmem((half, 2 * width), BF16),
            vmem((half, cols, width), BF16),
            vmem((half, cols, width), BF16),
            vmem((mine, total, width), BF16),
            vmem((nr, mine, total, width), BF16),
            vmem((mine, rows * nr, width), BF16),
            vmem((half, cols, width), BF16),
            vmem((mine, total, width), BF16),
            vmem((mine, rows * nr, width), BF16),
            dma((nc, parts)), dma((nc, parts)),
            dma((nc, parts)), dma((nc, parts)),
            dma((nc, parts)), dma((nc, parts)),
            dma((2, nr, parts)), dma((nr, parts)),
            dma((parts,)), dma((parts,)), dma((nc, parts)),
        ],
        compiler_params=pltpu.CompilerParams(
            collective_id=0, has_side_effects=True, vmem_limit_bytes=48 * 1024 * 1024
        ),
    )(*[pltpu.with_memory_space_constraint(a, pltpu.HBM) for a in operands])


def solution(mesh):
    placed = (P("row", "chan", None), P(), P(), P(), P(), P(), P(), P(), P(), P(), P(), P())
    return jax.shard_map(
        functools.partial(local, mesh.shape["row"], mesh.shape["chan"]),
        mesh=mesh, in_specs=placed, out_specs=P("row", "chan", None), check_vma=False,
    )
```

```python
import functools
import math

import jax
import jax.numpy as jnp
from jax import lax
from jax.experimental import pallas as pl
from jax.experimental.pallas import tpu as pltpu
from jax.sharding import PartitionSpec as P

MESH = pl.DeviceIdType.MESH
F32 = jnp.float32
BF16 = jnp.bfloat16
epsilon = 1e-05


def contract(a, b, da, db):
    return lax.dot_general(a, b, (((da,), (db,)), ((), ())), preferred_element_type=F32)


def column(row_ref):
    width = row_ref.shape[1]
    return jnp.transpose(jnp.broadcast_to(row_ref[...], (width, width)))


def kernel(
    nr, nc, parts,
    *refs,
):
    operands, (updated,), held, rest = refs[:12], refs[12:13], refs[13:25], refs[25:]
    body(nr, nc, parts, operands, held, updated, *rest)


def body(
    nr, nc, parts, operands, held, updated,
    fetched, normed, stage, gates, mask, left_w, right_w, means, scales, gain, shift, out_w,
    left_send, right_send, left_all, right_all, cross_send, cross_all,
    left_far, far_send,
    ls, lr, rs, rr, xs, xr, zs, zr, fs, fr, gs,
):
    fetches = [
        pltpu.make_async_copy(source, target, fetched.at[n])
        for n, (source, target) in enumerate(zip(operands, held))
    ]
    for fetch in fetches:
        fetch.start()
    (pair, tile_mask, in_gain, in_shift, left_gate, left_proj, right_gate, right_proj,
     out_gain, out_shift, out_gate, out_proj) = held
    rows, cols, width = pair.shape
    half = width // 2
    mine = half // nc
    each = mine // parts
    tiles = tile_mask.shape[0]
    tile = rows * nr // tiles
    r = lax.axis_index("row")
    c = lax.axis_index("chan")

    first, last = r == 0, r == nr - 1
    inner = jnp.logical_not(first | last)
    share, split = nr // 2, nc // 2

    barrier = pltpu.get_barrier_semaphore()

    @pl.loop(1, nc)
    def _(d):
        pl.semaphore_signal(
            barrier, inc=1, device_id={"chan": lax.rem(c + d, nc)}, device_id_type=MESH
        )

    @pl.when(r > 0)
    def _():
        pl.semaphore_signal(barrier, inc=1, device_id={"row": r - 1}, device_id_type=MESH)

    @pl.when(r < nr - 1)
    def _():
        pl.semaphore_signal(barrier, inc=1, device_id={"row": r + 1}, device_id_type=MESH)

    def greet(row):
        @pl.loop(1, nc)
        def _(d):
            pl.semaphore_signal(
                barrier, inc=1, device_id={"row": row, "chan": lax.rem(c + d, nc)},
                device_id_type=MESH,
            )

    @pl.when(last & (c < split))
    def _():
        greet(r - 1)

    @pl.when(first & (c >= split))
    def _():
        greet(r + 1)

    for n in (0, 2, 3):
        fetches[n].wait()

    group = 8

    @pl.loop(0, rows // group, unroll=2)
    def _(g):
        v = pair[pl.ds(g * group, group)].astype(F32).reshape(group * cols, width)
        m = jnp.mean(v, axis=1, keepdims=True)
        s = jnp.mean(v * v, axis=1, keepdims=True)
        n = (v - m) * lax.rsqrt(s - m * m + epsilon) * in_gain[...] + in_shift[...]
        normed[pl.ds(pl.multiple_of(g * group * cols, group * cols), group * cols), :] = (
            n.astype(BF16).astype(F32)
        )

    for n in (1, 4, 5, 6, 7, 8, 9, 10, 11):
        fetches[n].wait()

    tm = tile_mask[...].astype(F32)
    ids = lax.broadcasted_iota(jnp.int32, (cols, tiles), 0) + c * cols
    low = lax.broadcasted_iota(jnp.int32, (cols, tiles), 1) * tile
    col_hot = jnp.where((ids >= low) & (ids < low + tile), 1.0, 0.0)
    lane_t = lax.broadcasted_iota(jnp.int32, (tiles, width), 1)
    ids = jnp.where(lane_t < half, lane_t, lane_t - half) + r * rows
    low = lax.broadcasted_iota(jnp.int32, (tiles, width), 0) * tile
    row_hot = jnp.where((ids >= low) & (ids < low + tile), 1.0, 0.0)
    mask[...] = contract(contract(col_hot, tm, 1, 1), row_hot, 1, 0)

    def paired(w_ref):
        t = jnp.transpose(w_ref[...].astype(F32))
        return jnp.concatenate([t[:half], t[half:]], axis=1).astype(BF16)

    right_w[:half] = paired(right_gate)
    right_w[half:] = paired(right_proj)
    left_w[:half] = paired(left_gate)
    left_w[half:] = paired(left_proj)

    def at_column(k):
        return normed[pl.ds(k, rows, stride=cols), :].astype(BF16)

    def edges(w_ref, send):
        w = w_ref[...]
        empty = jnp.zeros((rows, width), BF16)

        @pl.loop(0, cols, unroll=8)
        def _(k):
            n = at_column(k)
            both = jnp.concatenate(
                [jnp.concatenate([n, empty], axis=1), jnp.concatenate([empty, n], axis=1)], axis=0
            )
            pre = contract(w, both, 1, 1)
            edge = mask[pl.ds(k, 1), :] * jax.nn.sigmoid(pre[:half]) * pre[half:]
            stage[pl.ds(k, half, stride=cols), :] = edge

        @pl.loop(0, half // group)
        def _(g):
            at = pl.ds(pl.multiple_of(g * group * cols, group * cols), group * cols)
            send[pl.ds(g * group, group)] = stage[at, :].astype(BF16).reshape(group, cols, width)

    def part_of(q):
        return pl.ds(q * each, each)

    def right_copy(d, q):
        to = lax.rem(c + d, nc)
        return pltpu.make_async_remote_copy(
            src_ref=right_send.at[pl.ds(to * mine + q * each, each)],
            dst_ref=right_all.at[r, part_of(q), pl.ds(pl.multiple_of(c * cols, cols), cols), :],
            send_sem=rs, recv_sem=rr.at[q],
            device_id={"chan": to}, device_id_type=MESH,
        )

    def left_copy(d, q):
        to = lax.rem(c + d, nc)
        return pltpu.make_async_remote_copy(
            src_ref=left_send.at[pl.ds(to * mine + q * each, each)],
            dst_ref=left_all.at[part_of(q), pl.ds(pl.multiple_of(c * cols, cols), cols), :],
            send_sem=ls, recv_sem=lr.at[q],
            device_id={"chan": to}, device_id_type=MESH,
        )

    def cross_copy(d, q):
        to = lax.rem(c + d, nc)
        return pltpu.make_async_remote_copy(
            src_ref=cross_send.at[part_of(q), pl.ds(pl.multiple_of(to * cols, cols), cols), :],
            dst_ref=cross_all.at[pl.ds(c * mine + q * each, each)],
            send_sem=xs, recv_sem=xr.at[q],
            device_id={"chan": to}, device_id_type=MESH,
        )

    def row_copy(block, q, way):
        return pltpu.make_async_remote_copy(
            src_ref=right_all.at[block, part_of(q)],
            dst_ref=right_all.at[block, part_of(q)],
            send_sem=zs.at[way, block], recv_sem=zr.at[block, q],
            device_id={"row": r + 1 - 2 * way}, device_id_type=MESH,
        )

    def all_bytes(ref, send_sem, recv_sem):
        return pltpu.make_async_remote_copy(
            src_ref=ref, dst_ref=ref, send_sem=send_sem, recv_sem=recv_sem,
            device_id={"chan": lax.rem(c + 1, nc)}, device_id_type=MESH,
        )

    others = pl.ds(0, (nc - 1) * cols)

    def right_wait(q):
        all_bytes(right_all.at[r, part_of(q), others, :], rs, rr.at[q]).wait_recv()

    def left_wait(q):
        all_bytes(left_all.at[part_of(q), others, :], ls, lr.at[q]).wait_recv()

    def each_peer(act):
        @pl.loop(1, nc)
        def _(d):
            act(d)

    own_cols = pl.ds(pl.multiple_of(c * cols, cols), cols)

    edges(right_w, right_send)
    pl.semaphore_wait(
        barrier,
        nc - 1 + jnp.where(r > 0, 1, 0) + jnp.where(r < nr - 1, 1, 0)
        + jnp.where(r == nr - 2, split - jnp.where(c < split, 1, 0), 0)
        + jnp.where(r == 1, nc - split - jnp.where(c >= split, 1, 0), 0),
    )
    for q in range(parts):
        each_peer(lambda d: right_copy(d, q).start())
    right_all[r, :, own_cols, :] = right_send[pl.ds(c * mine, mine)]

    lane = lax.broadcasted_iota(jnp.int32, (rows, width), 1)

    def left_over(q, way):
        return pltpu.make_async_remote_copy(
            src_ref=left_all.at[part_of(q)], dst_ref=left_far.at[part_of(q)],
            send_sem=fs, recv_sem=fr.at[q],
            device_id={"row": r + 1 - 2 * way}, device_id_type=MESH,
        )

    def far_copy(d, q, way):
        to = lax.rem(c + d, nc)
        return pltpu.make_async_remote_copy(
            src_ref=far_send.at[part_of(q), pl.ds(pl.multiple_of(to * cols, cols), cols), :],
            dst_ref=cross_all.at[pl.ds(c * mine + q * each, each)],
            send_sem=gs, recv_sem=xr.at[q],
            device_id={"row": r + 1 - 2 * way, "chan": to}, device_id_type=MESH,
        )

    def each_far(way, act):
        @pl.loop(0, nc)
        def _(d):
            to = lax.rem(c + d, nc)

            @pl.when((to >= split) if way else (to < split))
            def _():
                act(d)

    def is_near(to):
        return inner | (last & (to >= split)) | (first & (to < split))

    def each_near(act):
        @pl.loop(1, nc)
        def _(d):
            @pl.when(is_near(lax.rem(c + d, nc)))
            def _():
                act(d)

    def multiply(q, start, stop, left, into):
        @pl.loop(start, stop, unroll=2)
        def _(b):
            for h in range(q * each, (q + 1) * each):
                both = contract(right_all[b, h], left[h], 0, 0)
                x = jnp.where(lane < half, both[:half], both[half:]).astype(BF16)
                into[h, pl.ds(pl.multiple_of(b * rows, rows), rows), :] = x

    def own_products(q):
        @pl.when(first)
        def _():
            multiply(q, 0, share, left_all, cross_send)

        @pl.when(last)
        def _():
            multiply(q, share, nr, left_all, cross_send)

        @pl.when(inner)
        def _():
            left_wait(q)
            multiply(q, 0, nr, left_all, cross_send)

        each_near(lambda d: cross_copy(d, q).start())

        @pl.when(is_near(c))
        def _():
            cross_all[pl.ds(c * mine + q * each, each)] = cross_send[part_of(q), own_cols, :]

    def far_products(q):
        @pl.when(r == 1)
        def _():
            left_over(q, 0).wait_recv()
            multiply(q, share, nr, left_far, far_send)
            each_far(1, lambda d: far_copy(d, q, 1).start())

        @pl.when(r == nr - 2)
        def _():
            left_over(q, 1).wait_recv()
            multiply(q, 0, share, left_far, far_send)
            each_far(0, lambda d: far_copy(d, q, 0).start())

    def pass_on(block, q, way, arrives):
        if way == 0:
            there = (block >= 0) & jnp.logical_not(last & (block < share))
            goes = (r < nr - 2) | ((r == nr - 2) & (block >= share))
        else:
            there = (block < nr) & jnp.logical_not(first & (block >= share))
            goes = (r > 1) | ((r == 1) & (block < share))

        @pl.when(there)
        def _():
            if arrives:
                row_copy(block, q, way).wait_recv()

            @pl.when(goes)
            def _():
                row_copy(block, q, way).start()

    def own_on(q):
        right_wait(q)
        pass_on(r, q, 0, False)
        pass_on(r, q, 1, False)

    @pl.loop(0, cols, unroll=8)
    def _(k):
        gates[k] = jax.nn.sigmoid(contract(at_column(k), out_gate[...], 1, 0))

    own_on(0)

    edges(left_w, left_send)
    for q in range(parts):
        each_peer(lambda d: left_copy(d, q).start())
    left_all[:, own_cols, :] = left_send[pl.ds(c * mine, mine)]

    lane_h = lax.broadcasted_iota(jnp.int32, (half, width), 1)
    g = column(out_gain)
    s = column(out_shift)
    gain[...] = jnp.where(lane_h < half, g[:half], g[half:])
    shift[...] = jnp.where(lane_h < half, s[:half], s[half:])
    out_w[...] = jnp.concatenate([out_proj[:half], out_proj[half:]], axis=1)

    @pl.when(first | last)
    def _():
        def left_on(q):
            left_wait(q)

            @pl.when(first)
            def _():
                left_over(q, 0).start()

            @pl.when(last)
            def _():
                left_over(q, 1).start()

        for q in range(1, parts):
            own_on(q)
            left_on(q - 1)
        left_on(parts - 1)

    for t in range(parts + nr - 1):
        if 0 < t < parts:
            @pl.when(inner)
            def _():
                own_on(t)
        for s in range(1, nr - 1):
            q = t - s
            if 0 <= q < parts:
                pass_on(r - s, q, 0, True)
                pass_on(r + s, q, 1, True)
        if 0 <= t - (nr - 2) < parts:
            own_products(t - (nr - 2))
        if t >= nr - 1:
            far_products(t - (nr - 1))

    total = jnp.zeros((cols, width), F32)
    squares = total
    for q in range(parts):
        @pl.when(is_near(c))
        def _():
            all_bytes(cross_all.at[pl.ds(0, (nc - 1) * each)], xs, xr.at[q]).wait_recv()

        @pl.when(jnp.logical_not(is_near(c)))
        def _():
            all_bytes(cross_all.at[pl.ds(0, nc * each)], xs, xr.at[q]).wait_recv()

        def add_up(p, sums):
            for e in range(each):
                h = p * mine + q * each + e
                x = cross_all[h].astype(F32)
                stage[pl.ds(pl.multiple_of(h * cols, cols), cols), :] = x
                sums = sums[0] + x, sums[1] + x * x
            return sums

        total, squares = lax.fori_loop(0, nc, add_up, (total, squares), unroll=4)

    total = total + pltpu.roll(total, half, 1)
    squares = squares + pltpu.roll(squares, half, 1)
    m = total / width
    means[...] = m
    scales[...] = lax.rsqrt(squares / width - m * m + epsilon)

    @pl.loop(0, cols, unroll=8)
    def _(j):
        x = stage[pl.ds(j, half, stride=cols), :]
        x = (x - means[pl.ds(j, 1), :]) * scales[pl.ds(j, 1), :] * gain[...] + shift[...]
        y = contract(x.astype(BF16), out_w[...], 0, 0)
        normed[pl.ds(j, rows, stride=cols), :] = gates[j] * (y[:half, :width] + y[half:, width:])

    @pl.loop(0, rows // group)
    def _(g):
        at = pl.ds(pl.multiple_of(g * group * cols, group * cols), group * cols)
        updated[pl.ds(g * group, group)] = normed[at, :].astype(BF16).reshape(group, cols, width)

    all_bytes(right_send.at[pl.ds(0, (nc - 1) * mine)], rs, rr.at[0]).wait_send()
    all_bytes(left_send.at[pl.ds(0, (nc - 1) * mine)], ls, lr.at[0]).wait_send()

    def products_sent(count):
        there = pl.ds(0, count * cols)
        all_bytes(cross_send.at[:, there, :], xs, xr.at[0]).wait_send()

    @pl.when(inner)
    def _():
        products_sent(nc - 1)

    @pl.when((first | last) & is_near(c))
    def _():
        products_sent(split - 1)

    @pl.when(jnp.logical_not(is_near(c)))
    def _():
        products_sent(split)

    @pl.when((r == 1) | (r == nr - 2))
    def _():
        all_bytes(far_send.at[:, pl.ds(0, split * cols), :], gs, xr.at[0]).wait_send()

    @pl.when(first | last)
    def _():
        all_bytes(left_all, fs, fr.at[0]).wait_send()

    @pl.loop(0, nr)
    def _(block):
        @pl.when((block <= r) & ((r < nr - 2) | ((r == nr - 2) & (block >= share))))
        def _():
            all_bytes(right_all.at[block], zs.at[0, block], zr.at[block, 0]).wait_send()

        @pl.when((block >= r) & ((r > 1) | ((r == 1) & (block < share))))
        def _():
            all_bytes(right_all.at[block], zs.at[1, block], zr.at[block, 0]).wait_send()


def local(nr, nc, pair, tile_mask, in_gain, in_shift, left_gate, left_proj, right_gate, right_proj,
          out_gain, out_shift, out_gate, out_proj):
    rows, cols, width = pair.shape
    half = width // 2
    assert rows == half and nr >= 4 and nr % 2 == 0 and nc % 2 == 0 and nc >= 4
    mine = half // nc
    parts = math.gcd(mine, 4)
    total = cols * nc
    dma = pltpu.SemaphoreType.DMA
    vmem = pltpu.VMEM
    operands = (
        pair, tile_mask, in_gain[None], in_shift[None], left_gate, left_proj, right_gate,
        right_proj, out_gain[None], out_shift[None], out_gate, out_proj,
    )
    return pl.pallas_call(
        functools.partial(kernel, nr, nc, parts),
        out_shape=jax.ShapeDtypeStruct(pair.shape, BF16),
        in_specs=[pl.BlockSpec(memory_space=pltpu.HBM)] * 12,
        out_specs=pl.BlockSpec(memory_space=pltpu.VMEM),
        scratch_shapes=[vmem(a.shape, a.dtype) for a in operands] + [
            dma((len(operands),)),
            vmem((rows * cols, width), F32),
            vmem((half * cols, width), F32),
            vmem((cols, rows, width), F32),
            vmem((cols, width), F32),
            vmem((width, 2 * width), BF16),
            vmem((width, 2 * width), BF16),
            vmem((cols, width), F32),
            vmem((cols, width), F32),
            vmem((half, width), F32),
            vmem((half, width), F32),
            vmem((half, 2 * width), BF16),
            vmem((half, cols, width), BF16),
            vmem((half, cols, width), BF16),
            vmem((mine, total, width), BF16),
            vmem((nr, mine, total, width), BF16),
            vmem((mine, rows * nr, width), BF16),
            vmem((half, cols, width), BF16),
            vmem((mine, total, width), BF16),
            vmem((mine, rows * nr, width), BF16),
            dma, dma((parts,)),
            dma, dma((parts,)),
            dma, dma((parts,)),
            dma((2, nr)), dma((nr, parts)),
            dma, dma((parts,)), dma,
        ],
        compiler_params=pltpu.CompilerParams(
            collective_id=0, has_side_effects=True, vmem_limit_bytes=48 * 1024 * 1024
        ),
    )(*[pltpu.with_memory_space_constraint(a, pltpu.HBM) for a in operands])


def solution(mesh):
    placed = (P("row", "chan", None), P(), P(), P(), P(), P(), P(), P(), P(), P(), P(), P())
    return jax.shard_map(
        functools.partial(local, mesh.shape["row"], mesh.shape["chan"]),
        mesh=mesh, in_specs=placed, out_specs=P("row", "chan", None), check_vma=False,
    )
```

```python
import functools

import jax
import jax.numpy as jnp
from jax import lax
from jax.experimental import pallas as pl
from jax.experimental.pallas import tpu as pltpu
from jax.sharding import PartitionSpec as P

MESH = pl.DeviceIdType.MESH
F32 = jnp.float32
BF16 = jnp.bfloat16
epsilon = 1e-05


def contract(a, b, da, db):
    return lax.dot_general(a, b, (((da,), (db,)), ((), ())), preferred_element_type=F32)


def column(row_ref):
    width = row_ref.shape[1]
    return jnp.transpose(jnp.broadcast_to(row_ref[...], (width, width)))


def kernel(
    nr, nc, sizes,
    *refs,
):
    operands, (updated,), held, rest = refs[:12], refs[12:13], refs[13:25], refs[25:]
    body(nr, nc, sizes, operands, held, updated, *rest)


def body(
    nr, nc, sizes, operands, held, updated,
    fetched, normed, stage, gates, mask, left_w, right_w, means, scales, gain, shift, out_w,
    left_send, right_send, left_all, right_all, cross_send, cross_all,
    left_far, far_send,
    ls, lr, rs, rr, xs, xr, zs, zr, fs, fr, gs,
):
    fetches = [
        pltpu.make_async_copy(source, target, fetched.at[n])
        for n, (source, target) in enumerate(zip(operands, held))
    ]
    for fetch in fetches:
        fetch.start()
    (pair, tile_mask, in_gain, in_shift, left_gate, left_proj, right_gate, right_proj,
     out_gain, out_shift, out_gate, out_proj) = held
    rows, cols, width = pair.shape
    half = width // 2
    mine = half // nc
    begins = [sum(sizes[:q]) for q in range(len(sizes))]
    parts = len(sizes)
    middle = parts // 2
    groups = [(0, begins[middle]), (begins[middle], mine - begins[middle])]
    tiles = tile_mask.shape[0]
    tile = rows * nr // tiles
    r = lax.axis_index("row")
    c = lax.axis_index("chan")

    first, last = r == 0, r == nr - 1
    inner = jnp.logical_not(first | last)
    share, split = nr // 2, nc // 2

    barrier = pltpu.get_barrier_semaphore()

    @pl.loop(1, nc)
    def _(d):
        pl.semaphore_signal(
            barrier, inc=1, device_id={"chan": lax.rem(c + d, nc)}, device_id_type=MESH
        )

    @pl.when(r > 0)
    def _():
        pl.semaphore_signal(barrier, inc=1, device_id={"row": r - 1}, device_id_type=MESH)

    @pl.when(r < nr - 1)
    def _():
        pl.semaphore_signal(barrier, inc=1, device_id={"row": r + 1}, device_id_type=MESH)

    def greet(row):
        @pl.loop(1, nc)
        def _(d):
            pl.semaphore_signal(
                barrier, inc=1, device_id={"row": row, "chan": lax.rem(c + d, nc)},
                device_id_type=MESH,
            )

    @pl.when(last & (c < split))
    def _():
        greet(r - 1)

    @pl.when(first & (c >= split))
    def _():
        greet(r + 1)

    for n in (0, 2, 3):
        fetches[n].wait()

    group = 8

    @pl.loop(0, rows // group, unroll=2)
    def _(g):
        v = pair[pl.ds(g * group, group)].astype(F32).reshape(group * cols, width)
        m = jnp.mean(v, axis=1, keepdims=True)
        s = jnp.mean(v * v, axis=1, keepdims=True)
        n = (v - m) * lax.rsqrt(s - m * m + epsilon) * in_gain[...] + in_shift[...]
        normed[pl.ds(pl.multiple_of(g * group * cols, group * cols), group * cols), :] = (
            n.astype(BF16).astype(F32)
        )

    for n in (1, 4, 5, 6, 7, 8, 9, 10, 11):
        fetches[n].wait()

    tm = tile_mask[...].astype(F32)
    ids = lax.broadcasted_iota(jnp.int32, (cols, tiles), 0) + c * cols
    low = lax.broadcasted_iota(jnp.int32, (cols, tiles), 1) * tile
    col_hot = jnp.where((ids >= low) & (ids < low + tile), 1.0, 0.0)
    lane_t = lax.broadcasted_iota(jnp.int32, (tiles, width), 1)
    ids = jnp.where(lane_t < half, lane_t, lane_t - half) + r * rows
    low = lax.broadcasted_iota(jnp.int32, (tiles, width), 0) * tile
    row_hot = jnp.where((ids >= low) & (ids < low + tile), 1.0, 0.0)
    mask[...] = contract(contract(col_hot, tm, 1, 1), row_hot, 1, 0)

    def paired(w_ref):
        t = jnp.transpose(w_ref[...].astype(F32))
        return jnp.concatenate([t[:half], t[half:]], axis=1).astype(BF16)

    right_w[:half] = paired(right_gate)
    right_w[half:] = paired(right_proj)

    def at_column(k):
        return normed[pl.ds(k, rows, stride=cols), :].astype(BF16)

    def edges(w_ref, send):
        w = w_ref[...]
        empty = jnp.zeros((rows, width), BF16)

        @pl.loop(0, cols, unroll=8)
        def _(k):
            n = at_column(k)
            both = jnp.concatenate(
                [jnp.concatenate([n, empty], axis=1), jnp.concatenate([empty, n], axis=1)], axis=0
            )
            pre = contract(w, both, 1, 1)
            edge = mask[pl.ds(k, 1), :] * jax.nn.sigmoid(pre[:half]) * pre[half:]
            stage[pl.ds(k, half, stride=cols), :] = edge

        @pl.loop(0, half // group)
        def _(g):
            at = pl.ds(pl.multiple_of(g * group * cols, group * cols), group * cols)
            send[pl.ds(g * group, group)] = stage[at, :].astype(BF16).reshape(group, cols, width)

    def part_of(q):
        return pl.ds(begins[q], sizes[q])

    def right_copy(d, q):
        to = lax.rem(c + d, nc)
        return pltpu.make_async_remote_copy(
            src_ref=right_send.at[pl.ds(to * mine + begins[q], sizes[q])],
            dst_ref=right_all.at[r, part_of(q), pl.ds(pl.multiple_of(c * cols, cols), cols), :],
            send_sem=rs, recv_sem=rr.at[q],
            device_id={"chan": to}, device_id_type=MESH,
        )

    def left_copy(d, n):
        to = lax.rem(c + d, nc)
        begin, size = groups[n]
        return pltpu.make_async_remote_copy(
            src_ref=left_send.at[pl.ds(to * mine + begin, size)],
            dst_ref=left_all.at[pl.ds(begin, size), pl.ds(pl.multiple_of(c * cols, cols), cols), :],
            send_sem=ls, recv_sem=lr.at[n],
            device_id={"chan": to}, device_id_type=MESH,
        )

    def cross_copy(d, q):
        to = lax.rem(c + d, nc)
        return pltpu.make_async_remote_copy(
            src_ref=cross_send.at[part_of(q), pl.ds(pl.multiple_of(to * cols, cols), cols), :],
            dst_ref=cross_all.at[pl.ds(c * mine + begins[q], sizes[q])],
            send_sem=xs, recv_sem=xr.at[q],
            device_id={"chan": to}, device_id_type=MESH,
        )

    def row_copy(block, q, way):
        return pltpu.make_async_remote_copy(
            src_ref=right_all.at[block, part_of(q)],
            dst_ref=right_all.at[block, part_of(q)],
            send_sem=zs.at[way, block], recv_sem=zr.at[block, q],
            device_id={"row": r + 1 - 2 * way}, device_id_type=MESH,
        )

    def all_bytes(ref, send_sem, recv_sem):
        return pltpu.make_async_remote_copy(
            src_ref=ref, dst_ref=ref, send_sem=send_sem, recv_sem=recv_sem,
            device_id={"chan": lax.rem(c + 1, nc)}, device_id_type=MESH,
        )

    others = pl.ds(0, (nc - 1) * cols)

    def right_wait(q):
        all_bytes(right_all.at[r, part_of(q), others, :], rs, rr.at[q]).wait_recv()

    def left_wait(q):
        for n, (begin, size) in enumerate(groups):
            if begins[q] == begin:
                all_bytes(left_all.at[pl.ds(begin, size), others, :], ls, lr.at[n]).wait_recv()

    def each_peer(act):
        @pl.loop(1, nc)
        def _(d):
            act(d)

    own_cols = pl.ds(pl.multiple_of(c * cols, cols), cols)

    edges(right_w, right_send)
    pl.semaphore_wait(
        barrier,
        nc - 1 + jnp.where(r > 0, 1, 0) + jnp.where(r < nr - 1, 1, 0)
        + jnp.where(r == nr - 2, split - jnp.where(c < split, 1, 0), 0)
        + jnp.where(r == 1, nc - split - jnp.where(c >= split, 1, 0), 0),
    )
    for q in range(parts):
        each_peer(lambda d: right_copy(d, q).start())
    left_w[:half] = paired(left_gate)
    left_w[half:] = paired(left_proj)
    right_all[r, :, own_cols, :] = right_send[pl.ds(c * mine, mine)]

    lane = lax.broadcasted_iota(jnp.int32, (rows, width), 1)

    def left_over(q, way):
        return pltpu.make_async_remote_copy(
            src_ref=left_all.at[part_of(q)], dst_ref=left_far.at[part_of(q)],
            send_sem=fs, recv_sem=fr.at[q],
            device_id={"row": r + 1 - 2 * way}, device_id_type=MESH,
        )

    def far_copy(d, q, way):
        to = lax.rem(c + d, nc)
        return pltpu.make_async_remote_copy(
            src_ref=far_send.at[part_of(q), pl.ds(pl.multiple_of(to * cols, cols), cols), :],
            dst_ref=cross_all.at[pl.ds(c * mine + begins[q], sizes[q])],
            send_sem=gs, recv_sem=xr.at[q],
            device_id={"row": r + 1 - 2 * way, "chan": to}, device_id_type=MESH,
        )

    def each_far(way, act):
        @pl.loop(0, nc)
        def _(d):
            to = lax.rem(c + d, nc)

            @pl.when((to >= split) if way else (to < split))
            def _():
                act(d)

    def is_near(to):
        return inner | (last & (to >= split)) | (first & (to < split))

    def each_near(act):
        @pl.loop(1, nc)
        def _(d):
            @pl.when(is_near(lax.rem(c + d, nc)))
            def _():
                act(d)

    def multiply(q, start, stop, left, into):
        @pl.loop(start, stop)
        def _(b):
            for h in range(begins[q], begins[q] + sizes[q]):
                both = contract(right_all[b, h], left[h], 0, 0)
                x = jnp.where(lane < half, both[:half], both[half:]).astype(BF16)
                into[h, pl.ds(pl.multiple_of(b * rows, rows), rows), :] = x

    def early_products(q):
        @pl.when(first)
        def _():
            multiply(q, 0, share, left_all, cross_send)

        @pl.when(last)
        def _():
            multiply(q, share, nr, left_all, cross_send)

        @pl.when(inner)
        def _():
            left_wait(q)
            multiply(q, jnp.where(r == nr - 2, 1, 0), nr - jnp.where(r == 1, 1, 0), left_all, cross_send)

        @pl.when(first | last)
        def _():
            send_products(q)

    def late_products(q):
        @pl.when(r == 1)
        def _():
            multiply(q, nr - 1, nr, left_all, cross_send)

        @pl.when(r == nr - 2)
        def _():
            multiply(q, 0, 1, left_all, cross_send)

        @pl.when(inner)
        def _():
            send_products(q)

    def send_products(q):
        each_near(lambda d: cross_copy(d, q).start())

        @pl.when(is_near(c))
        def _():
            cross_all[pl.ds(c * mine + begins[q], sizes[q])] = cross_send[part_of(q), own_cols, :]

    def far_products(q):
        @pl.when(r == 1)
        def _():
            left_over(q, 0).wait_recv()
            multiply(q, share, nr, left_far, far_send)
            each_far(1, lambda d: far_copy(d, q, 1).start())

        @pl.when(r == nr - 2)
        def _():
            left_over(q, 1).wait_recv()
            multiply(q, 0, share, left_far, far_send)
            each_far(0, lambda d: far_copy(d, q, 0).start())

    def pass_on(block, q, way, arrives):
        if way == 0:
            there = (block >= 0) & jnp.logical_not(last & (block < share))
            goes = (r < nr - 2) | ((r == nr - 2) & (block >= share))
        else:
            there = (block < nr) & jnp.logical_not(first & (block >= share))
            goes = (r > 1) | ((r == 1) & (block < share))

        @pl.when(there)
        def _():
            if arrives:
                row_copy(block, q, way).wait_recv()

            @pl.when(goes)
            def _():
                row_copy(block, q, way).start()

    def own_on(q):
        right_wait(q)
        pass_on(r, q, 0, False)
        pass_on(r, q, 1, False)

    @pl.loop(0, cols, unroll=8)
    def _(k):
        gates[k] = jax.nn.sigmoid(contract(at_column(k), out_gate[...], 1, 0))

    own_on(0)

    edges(left_w, left_send)
    for n in range(len(groups)):
        each_peer(lambda d: left_copy(d, n).start())
    left_all[:, own_cols, :] = left_send[pl.ds(c * mine, mine)]

    lane_h = lax.broadcasted_iota(jnp.int32, (half, width), 1)
    g = column(out_gain)
    s = column(out_shift)
    gain[...] = jnp.where(lane_h < half, g[:half], g[half:])
    shift[...] = jnp.where(lane_h < half, s[:half], s[half:])
    out_w[...] = jnp.concatenate([out_proj[:half], out_proj[half:]], axis=1)

    @pl.when(first | last)
    def _():
        def left_on(q):
            left_wait(q)

            @pl.when(first)
            def _():
                left_over(q, 0).start()

            @pl.when(last)
            def _():
                left_over(q, 1).start()

        for q in range(1, parts):
            own_on(q)
            left_on(q - 1)
        left_on(parts - 1)

    for t in range(parts + nr - 2):
        if 0 < t < parts:
            @pl.when(inner)
            def _():
                own_on(t)
        for s in range(1, nr - 1):
            q = t - s
            if 0 <= q < parts:
                pass_on(r - s, q, 0, True)
                pass_on(r + s, q, 1, True)
        if t >= nr - 2:
            far_products(t - (nr - 2))
            late_products(t - (nr - 2))
        if 0 <= t - (nr - 3) < parts:
            early_products(t - (nr - 3))

    total = jnp.zeros((cols, width), F32)
    squares = total
    for q in range(parts):
        @pl.when(is_near(c))
        def _():
            all_bytes(cross_all.at[pl.ds(0, (nc - 1) * sizes[q])], xs, xr.at[q]).wait_recv()

        @pl.when(jnp.logical_not(is_near(c)))
        def _():
            all_bytes(cross_all.at[pl.ds(0, nc * sizes[q])], xs, xr.at[q]).wait_recv()

        def add_up(p, sums):
            for e in range(sizes[q]):
                h = p * mine + begins[q] + e
                x = cross_all[h].astype(F32)
                stage[pl.ds(pl.multiple_of(h * cols, cols), cols), :] = x
                sums = sums[0] + x, sums[1] + x * x
            return sums

        total, squares = lax.fori_loop(0, nc, add_up, (total, squares), unroll=4)

    total = total + pltpu.roll(total, half, 1)
    squares = squares + pltpu.roll(squares, half, 1)
    m = total / width
    means[...] = m
    scales[...] = lax.rsqrt(squares / width - m * m + epsilon)

    @pl.loop(0, cols, unroll=8)
    def _(j):
        x = stage[pl.ds(j, half, stride=cols), :]
        x = (x - means[pl.ds(j, 1), :]) * scales[pl.ds(j, 1), :] * gain[...] + shift[...]
        y = contract(x.astype(BF16), out_w[...], 0, 0)
        normed[pl.ds(j, rows, stride=cols), :] = gates[j] * (y[:half, :width] + y[half:, width:])

    @pl.loop(0, rows // group)
    def _(g):
        at = pl.ds(pl.multiple_of(g * group * cols, group * cols), group * cols)
        updated[pl.ds(g * group, group)] = normed[at, :].astype(BF16).reshape(group, cols, width)

    all_bytes(right_send.at[pl.ds(0, (nc - 1) * mine)], rs, rr.at[0]).wait_send()
    all_bytes(left_send.at[pl.ds(0, (nc - 1) * mine)], ls, lr.at[0]).wait_send()

    def products_sent(count):
        there = pl.ds(0, count * cols)
        all_bytes(cross_send.at[:, there, :], xs, xr.at[0]).wait_send()

    @pl.when(inner)
    def _():
        products_sent(nc - 1)

    @pl.when((first | last) & is_near(c))
    def _():
        products_sent(split - 1)

    @pl.when(jnp.logical_not(is_near(c)))
    def _():
        products_sent(split)

    @pl.when((r == 1) | (r == nr - 2))
    def _():
        all_bytes(far_send.at[:, pl.ds(0, split * cols), :], gs, xr.at[0]).wait_send()

    @pl.when(first | last)
    def _():
        all_bytes(left_all, fs, fr.at[0]).wait_send()

    @pl.loop(0, nr)
    def _(block):
        @pl.when((block <= r) & ((r < nr - 2) | ((r == nr - 2) & (block >= share))))
        def _():
            all_bytes(right_all.at[block], zs.at[0, block], zr.at[block, 0]).wait_send()

        @pl.when((block >= r) & ((r > 1) | ((r == 1) & (block < share))))
        def _():
            all_bytes(right_all.at[block], zs.at[1, block], zr.at[block, 0]).wait_send()


def local(nr, nc, pair, tile_mask, in_gain, in_shift, left_gate, left_proj, right_gate, right_proj,
          out_gain, out_shift, out_gate, out_proj):
    rows, cols, width = pair.shape
    half = width // 2
    mine = half // nc
    assert rows == half and nr >= 4 and nr % 2 == 0 and nc % 2 == 0 and nc >= 4 and mine >= 2
    sizes = (1,) * mine if mine < 4 else (1,) + (2,) * ((mine - 2) // 2) + (1,) * (1 + mine % 2)
    parts = len(sizes)
    total = cols * nc
    dma = pltpu.SemaphoreType.DMA
    vmem = pltpu.VMEM
    operands = (
        pair, tile_mask, in_gain[None], in_shift[None], left_gate, left_proj, right_gate,
        right_proj, out_gain[None], out_shift[None], out_gate, out_proj,
    )
    return pl.pallas_call(
        functools.partial(kernel, nr, nc, sizes),
        out_shape=jax.ShapeDtypeStruct(pair.shape, BF16),
        in_specs=[pl.BlockSpec(memory_space=pltpu.HBM)] * 12,
        out_specs=pl.BlockSpec(memory_space=pltpu.VMEM),
        scratch_shapes=[vmem(a.shape, a.dtype) for a in operands] + [
            dma((len(operands),)),
            vmem((rows * cols, width), F32),
            vmem((half * cols, width), F32),
            vmem((cols, rows, width), F32),
            vmem((cols, width), F32),
            vmem((width, 2 * width), BF16),
            vmem((width, 2 * width), BF16),
            vmem((cols, width), F32),
            vmem((cols, width), F32),
            vmem((half, width), F32),
            vmem((half, width), F32),
            vmem((half, 2 * width), BF16),
            vmem((half, cols, width), BF16),
            vmem((half, cols, width), BF16),
            vmem((mine, total, width), BF16),
            vmem((nr, mine, total, width), BF16),
            vmem((mine, rows * nr, width), BF16),
            vmem((half, cols, width), BF16),
            vmem((mine, total, width), BF16),
            vmem((mine, rows * nr, width), BF16),
            dma, dma((2,)),
            dma, dma((parts,)),
            dma, dma((parts,)),
            dma((2, nr)), dma((nr, parts)),
            dma, dma((parts,)), dma,
        ],
        compiler_params=pltpu.CompilerParams(
            collective_id=0, has_side_effects=True, vmem_limit_bytes=48 * 1024 * 1024
        ),
    )(*[pltpu.with_memory_space_constraint(a, pltpu.HBM) for a in operands])


def solution(mesh):
    placed = (P("row", "chan", None), P(), P(), P(), P(), P(), P(), P(), P(), P(), P(), P())
    return jax.shard_map(
        functools.partial(local, mesh.shape["row"], mesh.shape["chan"]),
        mesh=mesh, in_specs=placed, out_specs=P("row", "chan", None), check_vma=False,
    )
```

```python
import functools

import jax
import jax.numpy as jnp
from jax import lax
from jax.experimental import pallas as pl
from jax.experimental.pallas import tpu as pltpu
from jax.sharding import PartitionSpec as P

MESH = pl.DeviceIdType.MESH
F32 = jnp.float32
BF16 = jnp.bfloat16
epsilon = 1e-05


def contract(a, b, da, db):
    return lax.dot_general(a, b, (((da,), (db,)), ((), ())), preferred_element_type=F32)


def column(row_ref):
    width = row_ref.shape[1]
    return jnp.transpose(jnp.broadcast_to(row_ref[...], (width, width)))


def kernel(
    nr, nc, sizes,
    *refs,
):
    operands, (updated,), held, rest = refs[:12], refs[12:13], refs[13:25], refs[25:]
    body(nr, nc, sizes, operands, held, updated, *rest)


def body(
    nr, nc, sizes, operands, held, updated,
    fetched, normed, stage, gates, mask, left_w, right_w, means, scales, gain, shift, out_w,
    left_send, right_send, left_all, right_all, cross_send, cross_all,
    left_far, far_send,
    ls, lr, rs, rr, xs, xr, zs, zr, fs, fr, gs,
):
    fetches = [
        pltpu.make_async_copy(source, target, fetched.at[n])
        for n, (source, target) in enumerate(zip(operands, held))
    ]
    for fetch in fetches:
        fetch.start()
    (pair, tile_mask, in_gain, in_shift, left_gate, left_proj, right_gate, right_proj,
     out_gain, out_shift, out_gate, out_proj) = held
    rows, cols, width = pair.shape
    half = width // 2
    mine = half // nc
    begins = [sum(sizes[:q]) for q in range(len(sizes))]
    parts = len(sizes)
    middle = parts // 2
    groups = [(0, begins[middle]), (begins[middle], mine - begins[middle])]
    tiles = tile_mask.shape[0]
    tile = rows * nr // tiles
    r = lax.axis_index("row")
    c = lax.axis_index("chan")

    first, last = r == 0, r == nr - 1
    inner = jnp.logical_not(first | last)
    share, split = nr // 2, nc // 2

    barrier = pltpu.get_barrier_semaphore()

    @pl.loop(1, nc)
    def _(d):
        pl.semaphore_signal(
            barrier, inc=1, device_id={"chan": lax.rem(c + d, nc)}, device_id_type=MESH
        )

    @pl.when(r > 0)
    def _():
        pl.semaphore_signal(barrier, inc=1, device_id={"row": r - 1}, device_id_type=MESH)

    @pl.when(r < nr - 1)
    def _():
        pl.semaphore_signal(barrier, inc=1, device_id={"row": r + 1}, device_id_type=MESH)

    def greet(row):
        @pl.loop(1, nc)
        def _(d):
            pl.semaphore_signal(
                barrier, inc=1, device_id={"row": row, "chan": lax.rem(c + d, nc)},
                device_id_type=MESH,
            )

    @pl.when(last & (c < split))
    def _():
        greet(r - 1)

    @pl.when(first & (c >= split))
    def _():
        greet(r + 1)

    for n in (0, 2, 3):
        fetches[n].wait()

    group = 8

    @pl.loop(0, rows // group, unroll=2)
    def _(g):
        v = pair[pl.ds(g * group, group)].astype(F32).reshape(group * cols, width)
        m = jnp.mean(v, axis=1, keepdims=True)
        s = jnp.mean(v * v, axis=1, keepdims=True)
        n = (v - m) * lax.rsqrt(s - m * m + epsilon) * in_gain[...] + in_shift[...]
        normed[pl.ds(pl.multiple_of(g * group * cols, group * cols), group * cols), :] = (
            n.astype(BF16).astype(F32)
        )

    for n in (1, 4, 5, 6, 7, 8, 9, 10, 11):
        fetches[n].wait()

    tm = tile_mask[...].astype(F32)
    ids = lax.broadcasted_iota(jnp.int32, (cols, tiles), 0) + c * cols
    low = lax.broadcasted_iota(jnp.int32, (cols, tiles), 1) * tile
    col_hot = jnp.where((ids >= low) & (ids < low + tile), 1.0, 0.0)
    lane_t = lax.broadcasted_iota(jnp.int32, (tiles, width), 1)
    ids = jnp.where(lane_t < half, lane_t, lane_t - half) + r * rows
    low = lax.broadcasted_iota(jnp.int32, (tiles, width), 0) * tile
    row_hot = jnp.where((ids >= low) & (ids < low + tile), 1.0, 0.0)
    mask[...] = contract(contract(col_hot, tm, 1, 1), row_hot, 1, 0)

    def paired(w_ref):
        t = jnp.transpose(w_ref[...].astype(F32))
        return jnp.concatenate([t[:half], t[half:]], axis=1).astype(BF16)

    right_w[:half] = paired(right_gate)
    right_w[half:] = paired(right_proj)

    def at_column(k):
        return normed[pl.ds(k, rows, stride=cols), :].astype(BF16)

    def edges(w_ref, send):
        w = w_ref[...]
        empty = jnp.zeros((rows, width), BF16)

        @pl.loop(0, cols, unroll=8)
        def _(k):
            n = at_column(k)
            both = jnp.concatenate(
                [jnp.concatenate([n, empty], axis=1), jnp.concatenate([empty, n], axis=1)], axis=0
            )
            pre = contract(w, both, 1, 1)
            edge = mask[pl.ds(k, 1), :] * jax.nn.sigmoid(pre[:half]) * pre[half:]
            stage[pl.ds(k, half, stride=cols), :] = edge

        @pl.loop(0, half // group)
        def _(g):
            at = pl.ds(pl.multiple_of(g * group * cols, group * cols), group * cols)
            send[pl.ds(g * group, group)] = stage[at, :].astype(BF16).reshape(group, cols, width)

    def part_of(q):
        return pl.ds(begins[q], sizes[q])

    def right_copy(d, q):
        to = lax.rem(c + d, nc)
        return pltpu.make_async_remote_copy(
            src_ref=right_send.at[pl.ds(to * mine + begins[q], sizes[q])],
            dst_ref=right_all.at[r, part_of(q), pl.ds(pl.multiple_of(c * cols, cols), cols), :],
            send_sem=rs, recv_sem=rr.at[q],
            device_id={"chan": to}, device_id_type=MESH,
        )

    def left_copy(d, n):
        to = lax.rem(c + d, nc)
        begin, size = groups[n]
        return pltpu.make_async_remote_copy(
            src_ref=left_send.at[pl.ds(to * mine + begin, size)],
            dst_ref=left_all.at[pl.ds(begin, size), pl.ds(pl.multiple_of(c * cols, cols), cols), :],
            send_sem=ls, recv_sem=lr.at[n],
            device_id={"chan": to}, device_id_type=MESH,
        )

    def cross_copy(d, q):
        to = lax.rem(c + d, nc)
        return pltpu.make_async_remote_copy(
            src_ref=cross_send.at[part_of(q), pl.ds(pl.multiple_of(to * cols, cols), cols), :],
            dst_ref=cross_all.at[pl.ds(c * mine + begins[q], sizes[q])],
            send_sem=xs, recv_sem=xr.at[q],
            device_id={"chan": to}, device_id_type=MESH,
        )

    def row_copy(block, q, way):
        return pltpu.make_async_remote_copy(
            src_ref=right_all.at[block, part_of(q)],
            dst_ref=right_all.at[block, part_of(q)],
            send_sem=zs.at[way, block], recv_sem=zr.at[block, q],
            device_id={"row": r + 1 - 2 * way}, device_id_type=MESH,
        )

    def all_bytes(ref, send_sem, recv_sem):
        return pltpu.make_async_remote_copy(
            src_ref=ref, dst_ref=ref, send_sem=send_sem, recv_sem=recv_sem,
            device_id={"chan": lax.rem(c + 1, nc)}, device_id_type=MESH,
        )

    others = pl.ds(0, (nc - 1) * cols)

    def right_wait(q):
        all_bytes(right_all.at[r, part_of(q), others, :], rs, rr.at[q]).wait_recv()

    def left_wait(q):
        for n, (begin, size) in enumerate(groups):
            if begins[q] == begin:
                all_bytes(left_all.at[pl.ds(begin, size), others, :], ls, lr.at[n]).wait_recv()

    def each_peer(act):
        @pl.loop(1, nc)
        def _(d):
            act(d)

    own_cols = pl.ds(pl.multiple_of(c * cols, cols), cols)

    edges(right_w, right_send)
    pl.semaphore_wait(
        barrier,
        nc - 1 + jnp.where(r > 0, 1, 0) + jnp.where(r < nr - 1, 1, 0)
        + jnp.where(r == nr - 2, split - jnp.where(c < split, 1, 0), 0)
        + jnp.where(r == 1, nc - split - jnp.where(c >= split, 1, 0), 0),
    )
    for q in range(parts):
        each_peer(lambda d: right_copy(d, q).start())
    left_w[:half] = paired(left_gate)
    left_w[half:] = paired(left_proj)
    right_all[r, :, own_cols, :] = right_send[pl.ds(c * mine, mine)]

    lane = lax.broadcasted_iota(jnp.int32, (rows, width), 1)

    def left_over(q, way):
        return pltpu.make_async_remote_copy(
            src_ref=left_all.at[part_of(q)], dst_ref=left_far.at[part_of(q)],
            send_sem=fs, recv_sem=fr.at[q],
            device_id={"row": r + 1 - 2 * way}, device_id_type=MESH,
        )

    def far_copy(d, q, way):
        to = lax.rem(c + d, nc)
        return pltpu.make_async_remote_copy(
            src_ref=far_send.at[part_of(q), pl.ds(pl.multiple_of(to * cols, cols), cols), :],
            dst_ref=cross_all.at[pl.ds(c * mine + begins[q], sizes[q])],
            send_sem=gs, recv_sem=xr.at[q],
            device_id={"row": r + 1 - 2 * way, "chan": to}, device_id_type=MESH,
        )

    def each_far(way, act):
        @pl.loop(0, nc)
        def _(d):
            to = lax.rem(c + d, nc)

            @pl.when((to >= split) if way else (to < split))
            def _():
                act(d)

    def is_near(to):
        return inner | (last & (to >= split)) | (first & (to < split))

    def each_near(act):
        @pl.loop(1, nc)
        def _(d):
            @pl.when(is_near(lax.rem(c + d, nc)))
            def _():
                act(d)

    def multiply(q, start, stop, left, into):
        @pl.loop(start, stop)
        def _(b):
            for h in range(begins[q], begins[q] + sizes[q]):
                both = contract(right_all[b, h], left[h], 0, 0)
                x = jnp.where(lane < half, both[:half], both[half:]).astype(BF16)
                into[h, pl.ds(pl.multiple_of(b * rows, rows), rows), :] = x

    def early_products(q):
        @pl.when(first)
        def _():
            multiply(q, 0, share, left_all, cross_send)

        @pl.when(last)
        def _():
            multiply(q, share, nr, left_all, cross_send)

        @pl.when(inner)
        def _():
            left_wait(q)
            multiply(q, jnp.where(r == nr - 2, 1, 0), nr - jnp.where(r == 1, 1, 0), left_all, cross_send)

        @pl.when(first | last)
        def _():
            send_products(q)

    def late_products(q):
        @pl.when(r == 1)
        def _():
            multiply(q, nr - 1, nr, left_all, cross_send)

        @pl.when(r == nr - 2)
        def _():
            multiply(q, 0, 1, left_all, cross_send)

        @pl.when(inner)
        def _():
            send_products(q)

    def send_products(q):
        each_near(lambda d: cross_copy(d, q).start())

        @pl.when(is_near(c))
        def _():
            cross_all[pl.ds(c * mine + begins[q], sizes[q])] = cross_send[part_of(q), own_cols, :]

    def far_products(q):
        @pl.when(r == 1)
        def _():
            left_over(q, 0).wait_recv()
            multiply(q, share, nr, left_far, far_send)
            each_far(1, lambda d: far_copy(d, q, 1).start())

        @pl.when(r == nr - 2)
        def _():
            left_over(q, 1).wait_recv()
            multiply(q, 0, share, left_far, far_send)
            each_far(0, lambda d: far_copy(d, q, 0).start())

    def pass_on(block, q, way, arrives):
        if way == 0:
            there = (block >= 0) & jnp.logical_not(last & (block < share))
            goes = (r < nr - 2) | ((r == nr - 2) & (block >= share))
        else:
            there = (block < nr) & jnp.logical_not(first & (block >= share))
            goes = (r > 1) | ((r == 1) & (block < share))

        @pl.when(there)
        def _():
            if arrives:
                row_copy(block, q, way).wait_recv()

            @pl.when(goes)
            def _():
                row_copy(block, q, way).start()

    def own_on(q):
        right_wait(q)
        pass_on(r, q, 0, False)
        pass_on(r, q, 1, False)

    @pl.loop(0, cols, unroll=8)
    def _(k):
        gates[k] = jax.nn.sigmoid(contract(at_column(k), out_gate[...], 1, 0))

    own_on(0)

    edges(left_w, left_send)
    for n in range(len(groups)):
        each_peer(lambda d: left_copy(d, n).start())
    left_all[:, own_cols, :] = left_send[pl.ds(c * mine, mine)]

    for q in range(1, parts):
        own_on(q)

    lane_h = lax.broadcasted_iota(jnp.int32, (half, width), 1)
    g = column(out_gain)
    s = column(out_shift)
    gain[...] = jnp.where(lane_h < half, g[:half], g[half:])
    shift[...] = jnp.where(lane_h < half, s[:half], s[half:])
    out_w[...] = jnp.concatenate([out_proj[:half], out_proj[half:]], axis=1)

    @pl.when(first | last)
    def _():
        def left_on(q):
            left_wait(q)

            @pl.when(first)
            def _():
                left_over(q, 0).start()

            @pl.when(last)
            def _():
                left_over(q, 1).start()

        for q in range(parts):
            left_on(q)

    for s in range(1, nr - 1):
        for q in range(parts):
            pass_on(r - s, q, 0, True)
            pass_on(r + s, q, 1, True)
            if s == nr - 2:
                far_products(q)
                late_products(q)
        if s == nr - 3:
            for q in range(parts):
                early_products(q)

    total = jnp.zeros((cols, width), F32)
    squares = total
    for q in range(parts):
        @pl.when(is_near(c))
        def _():
            all_bytes(cross_all.at[pl.ds(0, (nc - 1) * sizes[q])], xs, xr.at[q]).wait_recv()

        @pl.when(jnp.logical_not(is_near(c)))
        def _():
            all_bytes(cross_all.at[pl.ds(0, nc * sizes[q])], xs, xr.at[q]).wait_recv()

        def add_up(p, sums):
            for e in range(sizes[q]):
                h = p * mine + begins[q] + e
                x = cross_all[h].astype(F32)
                stage[pl.ds(pl.multiple_of(h * cols, cols), cols), :] = x
                sums = sums[0] + x, sums[1] + x * x
            return sums

        total, squares = lax.fori_loop(0, nc, add_up, (total, squares), unroll=4)

    total = total + pltpu.roll(total, half, 1)
    squares = squares + pltpu.roll(squares, half, 1)
    m = total / width
    means[...] = m
    scales[...] = lax.rsqrt(squares / width - m * m + epsilon)

    @pl.loop(0, cols, unroll=8)
    def _(j):
        x = stage[pl.ds(j, half, stride=cols), :]
        x = (x - means[pl.ds(j, 1), :]) * scales[pl.ds(j, 1), :] * gain[...] + shift[...]
        y = contract(x.astype(BF16), out_w[...], 0, 0)
        normed[pl.ds(j, rows, stride=cols), :] = gates[j] * (y[:half, :width] + y[half:, width:])

    @pl.loop(0, rows // group)
    def _(g):
        at = pl.ds(pl.multiple_of(g * group * cols, group * cols), group * cols)
        updated[pl.ds(g * group, group)] = normed[at, :].astype(BF16).reshape(group, cols, width)

    all_bytes(right_send.at[pl.ds(0, (nc - 1) * mine)], rs, rr.at[0]).wait_send()
    all_bytes(left_send.at[pl.ds(0, (nc - 1) * mine)], ls, lr.at[0]).wait_send()

    def products_sent(count):
        there = pl.ds(0, count * cols)
        all_bytes(cross_send.at[:, there, :], xs, xr.at[0]).wait_send()

    @pl.when(inner)
    def _():
        products_sent(nc - 1)

    @pl.when((first | last) & is_near(c))
    def _():
        products_sent(split - 1)

    @pl.when(jnp.logical_not(is_near(c)))
    def _():
        products_sent(split)

    @pl.when((r == 1) | (r == nr - 2))
    def _():
        all_bytes(far_send.at[:, pl.ds(0, split * cols), :], gs, xr.at[0]).wait_send()

    @pl.when(first | last)
    def _():
        all_bytes(left_all, fs, fr.at[0]).wait_send()

    @pl.loop(0, nr)
    def _(block):
        @pl.when((block <= r) & ((r < nr - 2) | ((r == nr - 2) & (block >= share))))
        def _():
            all_bytes(right_all.at[block], zs.at[0, block], zr.at[block, 0]).wait_send()

        @pl.when((block >= r) & ((r > 1) | ((r == 1) & (block < share))))
        def _():
            all_bytes(right_all.at[block], zs.at[1, block], zr.at[block, 0]).wait_send()


def local(nr, nc, pair, tile_mask, in_gain, in_shift, left_gate, left_proj, right_gate, right_proj,
          out_gain, out_shift, out_gate, out_proj):
    rows, cols, width = pair.shape
    half = width // 2
    mine = half // nc
    assert rows == half and nr >= 4 and nr % 2 == 0 and nc % 2 == 0 and nc >= 4 and mine >= 2
    sizes = (1,) * mine if mine < 4 else (1,) + (2,) * ((mine - 2) // 2) + (1,) * (1 + mine % 2)
    parts = len(sizes)
    total = cols * nc
    dma = pltpu.SemaphoreType.DMA
    vmem = pltpu.VMEM
    operands = (
        pair, tile_mask, in_gain[None], in_shift[None], left_gate, left_proj, right_gate,
        right_proj, out_gain[None], out_shift[None], out_gate, out_proj,
    )
    return pl.pallas_call(
        functools.partial(kernel, nr, nc, sizes),
        out_shape=jax.ShapeDtypeStruct(pair.shape, BF16),
        in_specs=[pl.BlockSpec(memory_space=pltpu.HBM)] * 12,
        out_specs=pl.BlockSpec(memory_space=pltpu.VMEM),
        scratch_shapes=[vmem(a.shape, a.dtype) for a in operands] + [
            dma((len(operands),)),
            vmem((rows * cols, width), F32),
            vmem((half * cols, width), F32),
            vmem((cols, rows, width), F32),
            vmem((cols, width), F32),
            vmem((width, 2 * width), BF16),
            vmem((width, 2 * width), BF16),
            vmem((cols, width), F32),
            vmem((cols, width), F32),
            vmem((half, width), F32),
            vmem((half, width), F32),
            vmem((half, 2 * width), BF16),
            vmem((half, cols, width), BF16),
            vmem((half, cols, width), BF16),
            vmem((mine, total, width), BF16),
            vmem((nr, mine, total, width), BF16),
            vmem((mine, rows * nr, width), BF16),
            vmem((half, cols, width), BF16),
            vmem((mine, total, width), BF16),
            vmem((mine, rows * nr, width), BF16),
            dma, dma((2,)),
            dma, dma((parts,)),
            dma, dma((parts,)),
            dma((2, nr)), dma((nr, parts)),
            dma, dma((parts,)), dma,
        ],
        compiler_params=pltpu.CompilerParams(
            collective_id=0, has_side_effects=True, vmem_limit_bytes=48 * 1024 * 1024
        ),
    )(*[pltpu.with_memory_space_constraint(a, pltpu.HBM) for a in operands])


def solution(mesh):
    placed = (P("row", "chan", None), P(), P(), P(), P(), P(), P(), P(), P(), P(), P(), P())
    return jax.shard_map(
        functools.partial(local, mesh.shape["row"], mesh.shape["chan"]),
        mesh=mesh, in_specs=placed, out_specs=P("row", "chan", None), check_vma=False,
    )
```

```python
import functools

import jax
import jax.numpy as jnp
from jax import lax
from jax.experimental import pallas as pl
from jax.experimental.pallas import tpu as pltpu
from jax.sharding import PartitionSpec as P

MESH = pl.DeviceIdType.MESH
F32 = jnp.float32
BF16 = jnp.bfloat16
epsilon = 1e-05


def contract(a, b, da, db):
    return lax.dot_general(a, b, (((da,), (db,)), ((), ())), preferred_element_type=F32)


def column(row_ref):
    width = row_ref.shape[1]
    return jnp.transpose(jnp.broadcast_to(row_ref[...], (width, width)))


def kernel(
    nr, nc, sizes,
    *refs,
):
    operands, (updated,), held, rest = refs[:12], refs[12:13], refs[13:25], refs[25:]
    body(nr, nc, sizes, operands, held, updated, *rest)


def body(
    nr, nc, sizes, operands, held, updated,
    fetched, normed, stage, gates, mask, left_w, right_w, means, scales, gain, shift,
    left_send, right_send, left_all, right_all, cross_send, cross_all,
    left_far, far_send,
    ls, lr, rs, rr, xs, xr, zs, zr, fs, fr, gs,
):
    fetches = [
        pltpu.make_async_copy(source, target, fetched.at[n])
        for n, (source, target) in enumerate(zip(operands, held))
    ]
    for fetch in fetches:
        fetch.start()
    (pair, tile_mask, in_gain, in_shift, left_gate, left_proj, right_gate, right_proj,
     out_gain, out_shift, out_gate, out_proj) = held
    rows, cols, width = pair.shape
    half = width // 2
    mine = half // nc
    begins = [sum(sizes[:q]) for q in range(len(sizes))]
    parts = len(sizes)
    middle = parts // 2
    groups = [(0, begins[middle]), (begins[middle], mine - begins[middle])]
    tiles = tile_mask.shape[0]
    tile = rows * nr // tiles
    r = lax.axis_index("row")
    c = lax.axis_index("chan")

    first, last = r == 0, r == nr - 1
    inner = jnp.logical_not(first | last)
    share, split = nr // 2, nc // 2

    barrier = pltpu.get_barrier_semaphore()

    @pl.loop(1, nc)
    def _(d):
        pl.semaphore_signal(
            barrier, inc=1, device_id={"chan": lax.rem(c + d, nc)}, device_id_type=MESH
        )

    @pl.when(r > 0)
    def _():
        pl.semaphore_signal(barrier, inc=1, device_id={"row": r - 1}, device_id_type=MESH)

    @pl.when(r < nr - 1)
    def _():
        pl.semaphore_signal(barrier, inc=1, device_id={"row": r + 1}, device_id_type=MESH)

    def greet(row):
        @pl.loop(1, nc)
        def _(d):
            pl.semaphore_signal(
                barrier, inc=1, device_id={"row": row, "chan": lax.rem(c + d, nc)},
                device_id_type=MESH,
            )

    @pl.when(last & (c < split))
    def _():
        greet(r - 1)

    @pl.when(first & (c >= split))
    def _():
        greet(r + 1)

    for n in (0, 2, 3):
        fetches[n].wait()

    group = 8

    @pl.loop(0, rows // group, unroll=2)
    def _(g):
        v = pair[pl.ds(g * group, group)].astype(F32).reshape(group * cols, width)
        m = jnp.mean(v, axis=1, keepdims=True)
        s = jnp.mean(v * v, axis=1, keepdims=True)
        n = (v - m) * lax.rsqrt(s - m * m + epsilon) * in_gain[...] + in_shift[...]
        normed[pl.ds(pl.multiple_of(g * group * cols, group * cols), group * cols), :] = (
            n.astype(BF16).astype(F32)
        )

    for n in (1, 4, 5, 6, 7, 8, 9, 10, 11):
        fetches[n].wait()

    tm = tile_mask[...].astype(F32)
    ids = lax.broadcasted_iota(jnp.int32, (cols, tiles), 0) + c * cols
    low = lax.broadcasted_iota(jnp.int32, (cols, tiles), 1) * tile
    col_hot = jnp.where((ids >= low) & (ids < low + tile), 1.0, 0.0)
    lane_t = lax.broadcasted_iota(jnp.int32, (tiles, width), 1)
    ids = jnp.where(lane_t < half, lane_t, lane_t - half) + r * rows
    low = lax.broadcasted_iota(jnp.int32, (tiles, width), 0) * tile
    row_hot = jnp.where((ids >= low) & (ids < low + tile), 1.0, 0.0)
    mask[...] = contract(contract(col_hot, tm, 1, 1), row_hot, 1, 0)

    def turned(w_ref):
        return jnp.transpose(w_ref[...].astype(F32)).astype(BF16)

    right_w[:width] = turned(right_gate)
    right_w[width:] = turned(right_proj)

    lane = lax.broadcasted_iota(jnp.int32, (rows, width), 1)

    def swap(x, y):
        return (
            jnp.where(lane < half, x, pltpu.roll(y, half, 1)),
            jnp.where(lane < half, pltpu.roll(x, half, 1), y),
        )

    def at_column(k):
        return normed[pl.ds(k, rows, stride=cols), :].astype(BF16)

    def two_columns(k):
        return jnp.concatenate([at_column(k), at_column(k + 1)], axis=0)

    def edges(w_ref, send):
        w = w_ref[...]

        @pl.loop(0, cols // 2, unroll=4)
        def _(p):
            k = 2 * p
            pre = contract(w, two_columns(k), 1, 1)
            here = jnp.where(lane[:1] < half, mask[pl.ds(k, 1), :], mask[pl.ds(k + 1, 1), :])
            edge = here * jax.nn.sigmoid(pre[:width]) * pre[width:]
            one, two = swap(edge[:half], edge[half:])
            stage[pl.ds(k, half, stride=cols), :] = one
            stage[pl.ds(k + 1, half, stride=cols), :] = two

        @pl.loop(0, half // group)
        def _(g):
            at = pl.ds(pl.multiple_of(g * group * cols, group * cols), group * cols)
            send[pl.ds(g * group, group)] = stage[at, :].astype(BF16).reshape(group, cols, width)

    def part_of(q):
        return pl.ds(begins[q], sizes[q])

    def right_copy(d, q):
        to = lax.rem(c + d, nc)
        return pltpu.make_async_remote_copy(
            src_ref=right_send.at[pl.ds(to * mine + begins[q], sizes[q])],
            dst_ref=right_all.at[r, part_of(q), pl.ds(pl.multiple_of(c * cols, cols), cols), :],
            send_sem=rs, recv_sem=rr.at[q],
            device_id={"chan": to}, device_id_type=MESH,
        )

    def left_copy(d, n):
        to = lax.rem(c + d, nc)
        begin, size = groups[n]
        return pltpu.make_async_remote_copy(
            src_ref=left_send.at[pl.ds(to * mine + begin, size)],
            dst_ref=left_all.at[pl.ds(begin, size), pl.ds(pl.multiple_of(c * cols, cols), cols), :],
            send_sem=ls, recv_sem=lr.at[n],
            device_id={"chan": to}, device_id_type=MESH,
        )

    def cross_copy(d, q):
        to = lax.rem(c + d, nc)
        return pltpu.make_async_remote_copy(
            src_ref=cross_send.at[part_of(q), pl.ds(pl.multiple_of(to * cols, cols), cols), :],
            dst_ref=cross_all.at[pl.ds(c * mine + begins[q], sizes[q])],
            send_sem=xs, recv_sem=xr.at[q],
            device_id={"chan": to}, device_id_type=MESH,
        )

    def row_copy(block, q, way):
        return pltpu.make_async_remote_copy(
            src_ref=right_all.at[block, part_of(q)],
            dst_ref=right_all.at[block, part_of(q)],
            send_sem=zs.at[way, block], recv_sem=zr.at[block, q],
            device_id={"row": r + 1 - 2 * way}, device_id_type=MESH,
        )

    def all_bytes(ref, send_sem, recv_sem):
        return pltpu.make_async_remote_copy(
            src_ref=ref, dst_ref=ref, send_sem=send_sem, recv_sem=recv_sem,
            device_id={"chan": lax.rem(c + 1, nc)}, device_id_type=MESH,
        )

    others = pl.ds(0, (nc - 1) * cols)

    def right_wait(q):
        all_bytes(right_all.at[r, part_of(q), others, :], rs, rr.at[q]).wait_recv()

    def left_wait(q):
        for n, (begin, size) in enumerate(groups):
            if begins[q] == begin:
                all_bytes(left_all.at[pl.ds(begin, size), others, :], ls, lr.at[n]).wait_recv()

    def each_peer(act):
        @pl.loop(1, nc)
        def _(d):
            act(d)

    own_cols = pl.ds(pl.multiple_of(c * cols, cols), cols)

    edges(right_w, right_send)
    pl.semaphore_wait(
        barrier,
        nc - 1 + jnp.where(r > 0, 1, 0) + jnp.where(r < nr - 1, 1, 0)
        + jnp.where(r == nr - 2, split - jnp.where(c < split, 1, 0), 0)
        + jnp.where(r == 1, nc - split - jnp.where(c >= split, 1, 0), 0),
    )
    for q in range(parts):
        each_peer(lambda d: right_copy(d, q).start())
    left_w[:width] = turned(left_gate)
    left_w[width:] = turned(left_proj)
    right_all[r, :, own_cols, :] = right_send[pl.ds(c * mine, mine)]


    def left_over(q, way):
        return pltpu.make_async_remote_copy(
            src_ref=left_all.at[part_of(q)], dst_ref=left_far.at[part_of(q)],
            send_sem=fs, recv_sem=fr.at[q],
            device_id={"row": r + 1 - 2 * way}, device_id_type=MESH,
        )

    def far_copy(d, q, way):
        to = lax.rem(c + d, nc)
        return pltpu.make_async_remote_copy(
            src_ref=far_send.at[part_of(q), pl.ds(pl.multiple_of(to * cols, cols), cols), :],
            dst_ref=cross_all.at[pl.ds(c * mine + begins[q], sizes[q])],
            send_sem=gs, recv_sem=xr.at[q],
            device_id={"row": r + 1 - 2 * way, "chan": to}, device_id_type=MESH,
        )

    def each_far(way, act):
        @pl.loop(0, nc)
        def _(d):
            to = lax.rem(c + d, nc)

            @pl.when((to >= split) if way else (to < split))
            def _():
                act(d)

    def is_near(to):
        return inner | (last & (to >= split)) | (first & (to < split))

    def each_near(act):
        @pl.loop(1, nc)
        def _(d):
            @pl.when(is_near(lax.rem(c + d, nc)))
            def _():
                act(d)

    def multiply(q, start, stop, left, into):
        @pl.loop(start, stop)
        def _(b):
            for h in range(begins[q], begins[q] + sizes[q]):
                both = contract(right_all[b, h], left[h], 0, 0)
                x = jnp.where(lane < half, both[:half], both[half:]).astype(BF16)
                into[h, pl.ds(pl.multiple_of(b * rows, rows), rows), :] = x

    def early_products(q):
        @pl.when(first)
        def _():
            multiply(q, 0, share, left_all, cross_send)

        @pl.when(last)
        def _():
            multiply(q, share, nr, left_all, cross_send)

        @pl.when(inner)
        def _():
            left_wait(q)
            multiply(q, jnp.where(r == nr - 2, 1, 0), nr - jnp.where(r == 1, 1, 0), left_all, cross_send)

        @pl.when(first | last)
        def _():
            send_products(q)

    def late_products(q):
        @pl.when(r == 1)
        def _():
            multiply(q, nr - 1, nr, left_all, cross_send)

        @pl.when(r == nr - 2)
        def _():
            multiply(q, 0, 1, left_all, cross_send)

        @pl.when(inner)
        def _():
            send_products(q)

    def send_products(q):
        each_near(lambda d: cross_copy(d, q).start())

        @pl.when(is_near(c))
        def _():
            cross_all[pl.ds(c * mine + begins[q], sizes[q])] = cross_send[part_of(q), own_cols, :]

    def far_products(q):
        @pl.when(r == 1)
        def _():
            left_over(q, 0).wait_recv()
            multiply(q, share, nr, left_far, far_send)
            each_far(1, lambda d: far_copy(d, q, 1).start())

        @pl.when(r == nr - 2)
        def _():
            left_over(q, 1).wait_recv()
            multiply(q, 0, share, left_far, far_send)
            each_far(0, lambda d: far_copy(d, q, 0).start())

    def pass_on(block, q, way, arrives):
        if way == 0:
            there = (block >= 0) & jnp.logical_not(last & (block < share))
            goes = (r < nr - 2) | ((r == nr - 2) & (block >= share))
        else:
            there = (block < nr) & jnp.logical_not(first & (block >= share))
            goes = (r > 1) | ((r == 1) & (block < share))

        @pl.when(there)
        def _():
            if arrives:
                row_copy(block, q, way).wait_recv()

            @pl.when(goes)
            def _():
                row_copy(block, q, way).start()

    def own_on(q):
        right_wait(q)
        pass_on(r, q, 0, False)
        pass_on(r, q, 1, False)

    @pl.loop(0, cols // 2, unroll=4)
    def _(p):
        gates[p] = jax.nn.sigmoid(contract(two_columns(2 * p), out_gate[...], 1, 0))

    own_on(0)

    edges(left_w, left_send)
    for n in range(len(groups)):
        each_peer(lambda d: left_copy(d, n).start())
    left_all[:, own_cols, :] = left_send[pl.ds(c * mine, mine)]

    for q in range(1, parts):
        own_on(q)

    lane_h = lax.broadcasted_iota(jnp.int32, (half, width), 1)
    g = column(out_gain)
    s = column(out_shift)
    gain[...] = jnp.where(lane_h < half, g[:half], g[half:])
    shift[...] = jnp.where(lane_h < half, s[:half], s[half:])

    @pl.when(first | last)
    def _():
        def left_on(q):
            left_wait(q)

            @pl.when(first)
            def _():
                left_over(q, 0).start()

            @pl.when(last)
            def _():
                left_over(q, 1).start()

        for q in range(parts):
            left_on(q)

    for s in range(1, nr - 1):
        for q in range(parts):
            pass_on(r - s, q, 0, True)
            pass_on(r + s, q, 1, True)
            if s == nr - 2:
                far_products(q)
                late_products(q)
        if s == nr - 3:
            for q in range(parts):
                early_products(q)

    total = jnp.zeros((cols, width), F32)
    squares = total
    for q in range(parts):
        @pl.when(is_near(c))
        def _():
            all_bytes(cross_all.at[pl.ds(0, (nc - 1) * sizes[q])], xs, xr.at[q]).wait_recv()

        @pl.when(jnp.logical_not(is_near(c)))
        def _():
            all_bytes(cross_all.at[pl.ds(0, nc * sizes[q])], xs, xr.at[q]).wait_recv()

        def add_up(p, sums):
            for e in range(sizes[q]):
                h = p * mine + begins[q] + e
                x = cross_all[h].astype(F32)
                stage[pl.ds(pl.multiple_of(h * cols, cols), cols), :] = x
                sums = sums[0] + x, sums[1] + x * x
            return sums

        total, squares = lax.fori_loop(0, nc, add_up, (total, squares), unroll=4)

    total = total + pltpu.roll(total, half, 1)
    squares = squares + pltpu.roll(squares, half, 1)
    m = total / width
    means[...] = m
    scales[...] = lax.rsqrt(squares / width - m * m + epsilon)

    def normed_x(j):
        x = stage[pl.ds(j, half, stride=cols), :]
        return (x - means[pl.ds(j, 1), :]) * scales[pl.ds(j, 1), :] * gain[...] + shift[...]

    @pl.loop(0, cols // 2, unroll=4)
    def _(p):
        j = 2 * p
        low, high = swap(normed_x(j), normed_x(j + 1))
        x = jnp.concatenate([low, high], axis=0).astype(BF16)
        y = gates[p] * contract(x, out_proj[...], 0, 0)
        normed[pl.ds(j, rows, stride=cols), :] = y[:rows]
        normed[pl.ds(j + 1, rows, stride=cols), :] = y[rows:]

    @pl.loop(0, rows // group)
    def _(g):
        at = pl.ds(pl.multiple_of(g * group * cols, group * cols), group * cols)
        updated[pl.ds(g * group, group)] = normed[at, :].astype(BF16).reshape(group, cols, width)

    all_bytes(right_send.at[pl.ds(0, (nc - 1) * mine)], rs, rr.at[0]).wait_send()
    all_bytes(left_send.at[pl.ds(0, (nc - 1) * mine)], ls, lr.at[0]).wait_send()

    def products_sent(count):
        there = pl.ds(0, count * cols)
        all_bytes(cross_send.at[:, there, :], xs, xr.at[0]).wait_send()

    @pl.when(inner)
    def _():
        products_sent(nc - 1)

    @pl.when((first | last) & is_near(c))
    def _():
        products_sent(split - 1)

    @pl.when(jnp.logical_not(is_near(c)))
    def _():
        products_sent(split)

    @pl.when((r == 1) | (r == nr - 2))
    def _():
        all_bytes(far_send.at[:, pl.ds(0, split * cols), :], gs, xr.at[0]).wait_send()

    @pl.when(first | last)
    def _():
        all_bytes(left_all, fs, fr.at[0]).wait_send()

    @pl.loop(0, nr)
    def _(block):
        @pl.when((block <= r) & ((r < nr - 2) | ((r == nr - 2) & (block >= share))))
        def _():
            all_bytes(right_all.at[block], zs.at[0, block], zr.at[block, 0]).wait_send()

        @pl.when((block >= r) & ((r > 1) | ((r == 1) & (block < share))))
        def _():
            all_bytes(right_all.at[block], zs.at[1, block], zr.at[block, 0]).wait_send()


def local(nr, nc, pair, tile_mask, in_gain, in_shift, left_gate, left_proj, right_gate, right_proj,
          out_gain, out_shift, out_gate, out_proj):
    rows, cols, width = pair.shape
    half = width // 2
    mine = half // nc
    assert rows == half and cols % 2 == 0 and nr >= 4 and nr % 2 == 0 and nc % 2 == 0 and nc >= 4 and mine >= 2
    sizes = (1,) * mine if mine < 4 else (1,) + (2,) * ((mine - 2) // 2) + (1,) * (1 + mine % 2)
    parts = len(sizes)
    total = cols * nc
    dma = pltpu.SemaphoreType.DMA
    vmem = pltpu.VMEM
    operands = (
        pair, tile_mask, in_gain[None], in_shift[None], left_gate, left_proj, right_gate,
        right_proj, out_gain[None], out_shift[None], out_gate, out_proj,
    )
    return pl.pallas_call(
        functools.partial(kernel, nr, nc, sizes),
        out_shape=jax.ShapeDtypeStruct(pair.shape, BF16),
        in_specs=[pl.BlockSpec(memory_space=pltpu.HBM)] * 12,
        out_specs=pl.BlockSpec(memory_space=pltpu.VMEM),
        scratch_shapes=[vmem(a.shape, a.dtype) for a in operands] + [
            dma((len(operands),)),
            vmem((rows * cols, width), F32),
            vmem((half * cols, width), F32),
            vmem((cols // 2, 2 * rows, width), F32),
            vmem((cols, width), F32),
            vmem((2 * width, width), BF16),
            vmem((2 * width, width), BF16),
            vmem((cols, width), F32),
            vmem((cols, width), F32),
            vmem((half, width), F32),
            vmem((half, width), F32),
            vmem((half, cols, width), BF16),
            vmem((half, cols, width), BF16),
            vmem((mine, total, width), BF16),
            vmem((nr, mine, total, width), BF16),
            vmem((mine, rows * nr, width), BF16),
            vmem((half, cols, width), BF16),
            vmem((mine, total, width), BF16),
            vmem((mine, rows * nr, width), BF16),
            dma, dma((2,)),
            dma, dma((parts,)),
            dma, dma((parts,)),
            dma((2, nr)), dma((nr, parts)),
            dma, dma((parts,)), dma,
        ],
        compiler_params=pltpu.CompilerParams(
            collective_id=0, has_side_effects=True, vmem_limit_bytes=48 * 1024 * 1024
        ),
    )(*[pltpu.with_memory_space_constraint(a, pltpu.HBM) for a in operands])


def solution(mesh):
    placed = (P("row", "chan", None), P(), P(), P(), P(), P(), P(), P(), P(), P(), P(), P())
    return jax.shard_map(
        functools.partial(local, mesh.shape["row"], mesh.shape["chan"]),
        mesh=mesh, in_specs=placed, out_specs=P("row", "chan", None), check_vma=False,
    )
```
